256 devices in a mesh: seq: 64 (over x, z, y_hi), ch: 4 (over y_lo, core).
Axes of the slice: x: 4, y: 4 (y_hi: 2, y_lo: 2; y = y_hi * 2 + y_lo), z: 8, core: 2. Of those that a mesh axis runs over, the one named last changes fastest.
Arguments:
- bins_in: bfloat16 [65536, 1536], P('seq', 'ch'), may hold values from -6 to 6
- pre_scale: float32 [3, 1536], P(None, 'ch'), may hold values from 0.5 to 2
- pre_shift: float32 [3, 1536], P(None, 'ch'), may hold values from -1 to 1
- conv_weight: bfloat16 [3, 3, 1536, 1536], P(None, None, None, 'ch'), may hold values from -0.09375 to 0.09375
- conv_bias: float32 [3, 1536], P(None, 'ch'), may hold values from -0.5 to 0.5
Outputs:
- bins_out: bfloat16 [65536, 1536], P('seq', 'ch')
The draws below stay inside these ranges and needn't reach their ends.
All inputs are finite; a program needn't handle non-finite values.
Results may differ from the reference program's by a relative error of at most 0.015.
Values may be sent and summed in bfloat16 or wider, within the bound.
No kernel may reach another device: no remote copies, remote signals or barrier semaphores. Data moves between devices by JAX's collectives and lax.ppermute only.
A program may use at most 64 MiB of HBM per device.

```python
import math
import jax
import jax.numpy as jnp

C = 1536
LAYERS = 3
FIRST_SPACING1 = 64
SECOND_SPACING2 = 512
THIRD_SPACING3 = 4096
BINS = 65536


def shard_levels(key, extent, split, least, top_value):
    def one(dim, parts):
        heights = jax.random.uniform(jax.random.fold_in(jax.random.fold_in(key, 6), dim), (parts,), jnp.float32, least / len(split), top_value / len(split))
        return jnp.repeat(jnp.exp(heights), extent[dim] // parts).reshape((-1,) + (1,) * (len(extent) - dim - 1))

    gain = one(*split[0])
    for cut in split[1:]:
        gain = gain * one(*cut)
    return gain


def centred(stream_key, dims, deviation, limit, cuts=(), dtype=jnp.bfloat16):
    drawn = jax.random.normal(stream_key, dims, jnp.float32) * deviation
    if len(cuts) > 0:
        drawn = shard_levels(stream_key, dims, cuts, -0.22, 0.18) * drawn
    return jnp.clip(drawn, min=-limit, max=limit).astype(dtype)


def setup_inputs(seed: int = 0) -> dict:
    keys = jax.random.split(jax.random.key(seed), 6)
    bins_in = centred(keys[0], (BINS, C), 1.0, 6.0, ((0, 64), (1, 4)))
    pre_scale = jnp.clip(jnp.exp(math.log(2.0) - 1.3862944 * jax.random.uniform(keys[1], (LAYERS, C), jnp.float32) ** shard_levels(keys[1], (LAYERS, C), ((1, 4),), -0.2, 0.2)), 0.5, 2.0)
    pre_shift = jnp.clip(jax.random.uniform(keys[2], (LAYERS, C), jnp.float32, -1.0, 1.0) * shard_levels(keys[2], (LAYERS, C), ((1, 4),), -0.4, 0.0), -1.0, 1.0)
    conv_weight = centred(keys[3], (LAYERS, 3, C, C), (3 * C) ** -0.5, 0.09375, ((3, 4),))
    conv_bias = jnp.clip(jax.random.uniform(keys[4], (LAYERS, C), jnp.float32, -0.5, 0.5) * shard_levels(keys[4], (LAYERS, C), ((1, 4),), -0.4, 0.0), -0.5, 0.5)
    return dict(bins_in=bins_in, pre_scale=pre_scale, pre_shift=pre_shift, conv_weight=conv_weight, conv_bias=conv_bias)


def reference(bins_in, pre_scale, pre_shift, conv_weight, conv_bias):
    layer_spacings = (FIRST_SPACING1, SECOND_SPACING2, THIRD_SPACING3)
    stream = bins_in
    for layer_index in range(LAYERS):
        dilation = layer_spacings[layer_index]
        activated = jax.nn.gelu(stream.astype(jnp.float32) * pre_scale[layer_index] + pre_shift[layer_index], approximate=False).astype(jnp.bfloat16)
        padded = jnp.pad(activated, ((dilation, dilation), (0, 0)))
        summed = jnp.zeros((BINS, C), jnp.float32)
        for kernel_tap_index in range(3):
            window = padded[kernel_tap_index * dilation: kernel_tap_index * dilation + BINS]
            summed = summed + jnp.dot(window, conv_weight[layer_index, kernel_tap_index], preferred_element_type=jnp.float32)
        stream = (stream.astype(jnp.float32) + summed + conv_bias[layer_index]).astype(jnp.bfloat16)
    return stream
```

```python
import jax
import jax.numpy as jnp
from jax import lax
from jax.experimental import pallas as pl
from jax.experimental.pallas import tpu as pltpu
from jax.sharding import PartitionSpec as P

F32 = jnp.float32
BF16 = jnp.bfloat16
ERFC = (
    -1.26551223, 1.00002368, 0.37409196, 0.09678418, -0.18628806,
    0.27886807, -1.13520398, 1.48851587, -0.82215223, 0.17087277,
)
RIM = 64
FIRST = 576
VMEM = pl.BlockSpec(memory_space=pltpu.VMEM)
SMEM = pl.BlockSpec(memory_space=pltpu.SMEM)


def gelu(x):
    z = jnp.abs(x) * 0.7071067811865476
    t = 1.0 / (1.0 + 0.5 * z)
    poly = jnp.full_like(t, ERFC[-1])
    for c in ERFC[-2::-1]:
        poly = poly * t + c
    e = t * jnp.exp(poly - z * z)
    return 0.5 * x * jnp.where(x >= 0.0, 2.0 - e, e)


def shifted(array, by):
    size = lax.axis_size("seq")
    pairs = [(i, i + by) for i in range(size) if 0 <= i + by < size]
    return lax.ppermute(array, "seq", pairs)


def chip_swap(array):
    return lax.ppermute(array, "ch", [(i, i ^ 2) for i in range(4)])


def core_swap(array):
    return lax.ppermute(array, "ch", [(i, i ^ 1) for i in range(4)])


def gathered(own):
    far = chip_swap(own)
    return (own, core_swap(own), far, core_swap(far))


def place(ch_ref, pieces, rows, buf, at, count):
    width = pieces[0].shape[1]
    for p, piece in enumerate(pieces):
        j = ch_ref[0] ^ p
        col = pl.multiple_of(j * width, 128)
        buf[at : at + count, pl.ds(col, width)] = piece[rows : rows + count, :]


def taps(buf, w_ref, at, count):
    acc = jnp.dot(buf[at - RIM : at - RIM + count, :], w_ref[0, 0], preferred_element_type=F32)
    acc += jnp.dot(buf[at : at + count, :], w_ref[0, 1], preferred_element_type=F32)
    acc += jnp.dot(buf[at + RIM : at + RIM + count, :], w_ref[0, 2], preferred_element_type=F32)
    return acc


def finish(acc, bins, vec_ref, s_ref, a_ref, at, count):
    s = (bins.astype(F32) + acc + vec_ref[0:1, :]).astype(BF16)
    s_ref[at : at + count, :] = s
    a_ref[at : at + count, :] = gelu(s.astype(F32) * vec_ref[1:2, :] + vec_ref[2:3, :]).astype(BF16)


def first_kernel(ch_ref, p0, p1, p2, p3, w_ref, bins_ref, vec_ref, s_ref, a_ref, buf):
    place(ch_ref, (p0, p1, p2, p3), 0, buf, 0, FIRST)
    count = FIRST - 2 * RIM
    half = count // 2
    for at in (RIM, RIM + half):
        acc = taps(buf, w_ref, at, half)
        finish(acc, bins_ref[at : at + half, :], vec_ref, s_ref, a_ref, at - RIM, half)


def second_kernel(ch_ref, p0, p1, p2, p3, r0, r1, r2, r3, w_ref, bins_ref, vec_ref, s_ref, a_ref, buf):
    rows = bins_ref.shape[0]
    rest = rows - FIRST
    early, late = (p0, p1, p2, p3), (r0, r1, r2, r3)
    place(ch_ref, late, rest, buf, 0, RIM)
    place(ch_ref, early, 0, buf, RIM, FIRST)
    place(ch_ref, late, 0, buf, RIM + FIRST, rest)
    place(ch_ref, late, rest + RIM, buf, RIM + rows, RIM)
    acc = taps(buf, w_ref, RIM, RIM)
    finish(acc, bins_ref[:RIM, :], vec_ref, s_ref, a_ref, 0, RIM)
    start = FIRST - RIM
    half = (rows - start) // 2
    for i in range(2):
        at = start + i * half
        acc = taps(buf, w_ref, RIM + at, half)
        finish(acc, bins_ref[at : at + half, :], vec_ref, s_ref, a_ref, RIM + i * half, half)


def product_kernel(ch_ref, p0, p1, p2, p3, w_ref, o0, o1, o2, buf):
    rows = p0.shape[0]
    place(ch_ref, (p0, p1, p2, p3), 0, buf, 0, rows)
    for k, o in ((0, o0), (2, o2), (1, o1)):
        o[...] = jnp.dot(buf[...], w_ref[0, k], preferred_element_type=F32).astype(BF16)


def call(kernel, args, outs, scratch_rows, flops):
    width = outs[0][1]
    return pl.pallas_call(
        kernel,
        out_shape=[jax.ShapeDtypeStruct(o, BF16) for o in outs],
        in_specs=[SMEM] + [VMEM] * (len(args) - 1),
        out_specs=[VMEM] * len(outs),
        scratch_shapes=[pltpu.VMEM((scratch_rows, 4 * width), BF16)],
        compiler_params=pltpu.CompilerParams(vmem_limit_bytes=40 * 1024 * 1024),
        cost_estimate=pl.CostEstimate(flops=flops, bytes_accessed=8 * 1024 * 1024, transcendentals=0),
    )(*args)


def per_device(bins_in, pre_scale, pre_shift, conv_weight, conv_bias):
    rows, width = bins_in.shape
    ch = lax.axis_index("ch").astype(jnp.int32).reshape(1)
    hop1 = 1
    hop2 = 4096 // rows
    mac = 2 * 4 * width * width * 3

    act = gelu(bins_in.astype(F32) * pre_scale[0] + pre_shift[0]).astype(BF16)
    early = gathered(act[:FIRST])
    low = shifted(act[rows - RIM :], 1)
    high = shifted(act[:RIM], -1)
    late = gathered(jnp.concatenate([act[FIRST:], low, high], axis=0))

    vec0 = jnp.stack([conv_bias[0], pre_scale[1], pre_shift[1]])
    n0 = FIRST - 2 * RIM
    n1 = rows - n0
    s_x0, a_x0 = call(first_kernel, (ch, *early, conv_weight[0:1], bins_in, vec0), [(n0, width)] * 2, FIRST, mac * n0)
    g_x0 = gathered(a_x0)
    s_x1, a_x1 = call(
        second_kernel, (ch, *early, *late, conv_weight[0:1], bins_in, vec0), [(n1, width)] * 2, rows + 2 * RIM, mac * n1
    )
    g_x1 = gathered(a_x1)

    p0a, p1a, p2a = call(product_kernel, (ch, *g_x0, conv_weight[1:2]), [(n0, width)] * 3, n0, mac * n0)
    from_next_a = shifted(p2a, -hop1)
    p0b, p1b, p2b = call(product_kernel, (ch, *g_x1, conv_weight[1:2]), [(n1, width)] * 3, n1, mac * n1)
    from_next_b = shifted(p2b[:RIM], -hop1)
    from_prev = shifted(p0b[RIM:], hop1)

    f = lambda v: v.astype(F32)
    cat = lambda *v: jnp.concatenate([f(x) for x in v], axis=0)
    s2_hi = f(s_x1[RIM:]) + f(p1b[RIM:]) + cat(p0b[:RIM], p0a) + cat(from_next_b, from_next_a) + conv_bias[1]
    s2_hi = s2_hi.astype(BF16)
    a2_hi = gelu(f(s2_hi) * pre_scale[2] + pre_shift[2]).astype(BF16)
    g_hi = gathered(a2_hi)
    s2_lo = cat(s_x1[:RIM], s_x0) + cat(p1b[:RIM], p1a) + f(p2b[RIM:]) + f(from_prev) + conv_bias[1]
    s2_lo = s2_lo.astype(BF16)
    a2_lo = gelu(f(s2_lo) * pre_scale[2] + pre_shift[2]).astype(BF16)
    g_lo = gathered(a2_lo)

    out = []
    for g, s2 in ((g_hi, s2_hi), (g_lo, s2_lo)):
        q0, q1, q2 = call(product_kernel, (ch, *g, conv_weight[2:3]), [s2.shape] * 3, s2.shape[0], mac * s2.shape[0])
        up = shifted(q0, hop2)
        down = shifted(q2, -hop2)
        out.append((f(s2) + f(q1) + f(up) + f(down) + conv_bias[2]).astype(BF16))
    return jnp.concatenate([out[1], out[0]], axis=0)


def solution(mesh):
    return jax.shard_map(
        per_device,
        mesh=mesh,
        in_specs=(
            P("seq", "ch"),
            P(None, "ch"),
            P(None, "ch"),
            P(None, None, None, "ch"),
            P(None, "ch"),
        ),
        out_specs=P("seq", "ch"),
        check_vma=False,
    )
```

```python
import functools

import jax
import jax.numpy as jnp
from jax import lax
from jax.experimental import pallas as pl
from jax.experimental.pallas import tpu as pltpu
from jax.sharding import PartitionSpec as P

F32 = jnp.float32
BF16 = jnp.bfloat16
ERFC = (
    -1.26551223, 1.00002368, 0.37409196, 0.09678418, -0.18628806,
    0.27886807, -1.13520398, 1.48851587, -0.82215223, 0.17087277,
)
RIM = 64
FIRST = 576
VMEM = pl.BlockSpec(memory_space=pltpu.VMEM)
SMEM = pl.BlockSpec(memory_space=pltpu.SMEM)


def gelu(x):
    z = jnp.abs(x) * 0.7071067811865476
    t = 1.0 / (1.0 + 0.5 * z)
    poly = jnp.full_like(t, ERFC[-1])
    for c in ERFC[-2::-1]:
        poly = poly * t + c
    e = t * jnp.exp(poly - z * z)
    return 0.5 * x * jnp.where(x >= 0.0, 2.0 - e, e)


def shifted(array, by):
    size = lax.axis_size("seq")
    pairs = [(i, i + by) for i in range(size) if 0 <= i + by < size]
    return lax.ppermute(array, "seq", pairs)


def chip_swap(array):
    return lax.ppermute(array, "ch", [(i, i ^ 2) for i in range(4)])


def core_swap(array):
    return lax.ppermute(array, "ch", [(i, i ^ 1) for i in range(4)])


def gathered(own):
    far = chip_swap(own)
    return (own, core_swap(own), far, core_swap(far))


def place(ch_ref, pieces, rows, buf, at, count):
    width = pieces[0].shape[1]
    for p, piece in enumerate(pieces):
        j = ch_ref[0] ^ p
        col = pl.multiple_of(j * width, 128)
        buf[at : at + count, pl.ds(col, width)] = piece[rows : rows + count, :]


def fetch(layer, w_hbm, w_ref, sems):
    copies = [pltpu.make_async_copy(w_hbm.at[layer, k], w_ref.at[k], sems.at[k]) for k in range(3)]
    for copy in copies:
        copy.start()
    return copies


def tap(buf, w_ref, k, at, count):
    lo = at + (k - 1) * RIM
    return jnp.dot(buf[lo : lo + count, :], w_ref[k], preferred_element_type=F32)


def finish(acc, bins, vec_ref, s_ref, a_ref, at, count):
    s = (bins.astype(F32) + acc + vec_ref[0:1, :]).astype(BF16)
    s_ref[at : at + count, :] = s
    a_ref[at : at + count, :] = gelu(s.astype(F32) * vec_ref[1:2, :] + vec_ref[2:3, :]).astype(BF16)


def first_kernel(ch_ref, p0, p1, p2, p3, bins_ref, vec_ref, w_hbm, s_ref, a_ref, buf, w_ref, sems):
    copies = fetch(0, w_hbm, w_ref, sems)
    place(ch_ref, (p0, p1, p2, p3), 0, buf, 0, FIRST)
    for copy in copies:
        copy.wait()
    count = FIRST - 2 * RIM
    half = count // 2
    for at in (RIM, RIM + half):
        acc = tap(buf, w_ref, 0, at, half) + tap(buf, w_ref, 1, at, half) + tap(buf, w_ref, 2, at, half)
        finish(acc, bins_ref[at : at + half, :], vec_ref, s_ref, a_ref, at - RIM, half)


def second_kernel(ch_ref, p0, p1, p2, p3, r0, r1, r2, r3, bins_ref, vec_ref, w_hbm, s_ref, a_ref, buf, w_ref, sems):
    copies = fetch(0, w_hbm, w_ref, sems)
    rows = bins_ref.shape[0]
    rest = rows - FIRST
    early, late = (p0, p1, p2, p3), (r0, r1, r2, r3)
    place(ch_ref, late, rest, buf, 0, RIM)
    place(ch_ref, early, 0, buf, RIM, FIRST)
    place(ch_ref, late, 0, buf, RIM + FIRST, rest)
    place(ch_ref, late, rest + RIM, buf, RIM + rows, RIM)
    for copy in copies:
        copy.wait()
    start = FIRST - RIM
    half = (rows - start) // 2
    for at, to, count in ((0, 0, RIM), (start, RIM, half), (start + half, RIM + half, half)):
        lo = RIM + at
        acc = tap(buf, w_ref, 0, lo, count) + tap(buf, w_ref, 1, lo, count) + tap(buf, w_ref, 2, lo, count)
        finish(acc, bins_ref[at : at + count, :], vec_ref, s_ref, a_ref, to, count)


def product_kernel(layer, ch_ref, p0, p1, p2, p3, w_hbm, o0, o1, o2, buf, w_ref, sems):
    copies = fetch(layer, w_hbm, w_ref, sems)
    rows = p0.shape[0]
    place(ch_ref, (p0, p1, p2, p3), 0, buf, 0, rows)
    for k, o in ((0, o0), (1, o1), (2, o2)):
        copies[k].wait()
        o[...] = jnp.dot(buf[...], w_ref[k], preferred_element_type=F32).astype(BF16)


def call(kernel, args, outs, scratch_rows, flops):
    width = outs[0][1]
    return pl.pallas_call(
        kernel,
        out_shape=[jax.ShapeDtypeStruct(o, BF16) for o in outs],
        in_specs=[SMEM] + [VMEM] * (len(args) - 2) + [pl.BlockSpec(memory_space=pltpu.HBM)],
        out_specs=[VMEM] * len(outs),
        scratch_shapes=[
            pltpu.VMEM((scratch_rows, 4 * width), BF16),
            pltpu.VMEM((3, 4 * width, width), BF16),
            pltpu.SemaphoreType.DMA((3,)),
        ],
        compiler_params=pltpu.CompilerParams(vmem_limit_bytes=28 * 1024 * 1024),
        cost_estimate=pl.CostEstimate(flops=flops, bytes_accessed=8 * 1024 * 1024, transcendentals=0),
    )(*args)


def per_device(bins_in, pre_scale, pre_shift, conv_weight, conv_bias):
    rows, width = bins_in.shape
    ch = lax.axis_index("ch").astype(jnp.int32).reshape(1)
    hop1 = 1
    hop2 = 4096 // rows
    mac = 2 * 4 * width * width * 3

    f = lambda v: v.astype(F32)
    cat = lambda *v: jnp.concatenate([f(x) for x in v], axis=0)
    products1 = functools.partial(product_kernel, 1)
    products2 = functools.partial(product_kernel, 2)

    def entry(x):
        return gelu(f(x) * pre_scale[0] + pre_shift[0]).astype(BF16)

    act_early = entry(bins_in[:FIRST])
    far_early = chip_swap(act_early)
    act_late = entry(bins_in[FIRST:])
    low = shifted(act_late[-RIM:], 1)
    high = shifted(act_early[:RIM], -1)
    near_early = core_swap(act_early)
    own_late = jnp.concatenate([act_late, low, high], axis=0)
    far_late = chip_swap(own_late)
    near_late = core_swap(own_late)
    early = (act_early, near_early, far_early, core_swap(far_early))

    vec0 = jnp.stack([conv_bias[0], pre_scale[1], pre_shift[1]])
    n0 = FIRST - 2 * RIM
    n1 = rows - n0
    s_x0, a_x0 = call(first_kernel, (ch, *early, bins_in, vec0, conv_weight), [(n0, width)] * 2, FIRST, mac * n0)
    far_x0 = chip_swap(a_x0)
    near_x0 = core_swap(a_x0)
    far_late, a_x0 = lax.optimization_barrier((far_late, a_x0))
    late = (own_late, near_late, far_late, core_swap(far_late))
    s_x1, a_x1 = call(
        second_kernel, (ch, *early, *late, bins_in, vec0, conv_weight), [(n1, width)] * 2, rows + 2 * RIM, mac * n1
    )
    far_x1 = chip_swap(a_x1)
    near_x1 = core_swap(a_x1)
    far_x0, a_x1 = lax.optimization_barrier((far_x0, a_x1))
    g_x0 = (a_x0, near_x0, far_x0, core_swap(far_x0))
    p0a, p1a, p2a = call(products1, (ch, *g_x0, conv_weight), [(n0, width)] * 3, n0, mac * n0)
    from_next_a = shifted(p2a, -hop1)
    far_x1, p0a = lax.optimization_barrier((far_x1, p0a))
    g_x1 = (a_x1, near_x1, far_x1, core_swap(far_x1))
    p0b, p1b, p2b = call(products1, (ch, *g_x1, conv_weight), [(n1, width)] * 3, n1, mac * n1)
    from_next_b = shifted(p2b[:RIM], -hop1)
    from_prev = shifted(p0b[RIM:], hop1)

    s2_hi = f(s_x1[RIM:]) + f(p1b[RIM:]) + cat(p0b[:RIM], p0a) + cat(from_next_b, from_next_a) + conv_bias[1]
    s2_hi = s2_hi.astype(BF16)
    a2_hi = gelu(f(s2_hi) * pre_scale[2] + pre_shift[2]).astype(BF16)
    far_hi = chip_swap(a2_hi)
    near_hi = core_swap(a2_hi)
    from_prev, a2_hi = lax.optimization_barrier((from_prev, a2_hi))
    s2_lo = cat(s_x1[:RIM], s_x0) + cat(p1b[:RIM], p1a) + f(p2b[RIM:]) + f(from_prev) + conv_bias[1]
    s2_lo = s2_lo.astype(BF16)
    a2_lo = gelu(f(s2_lo) * pre_scale[2] + pre_shift[2]).astype(BF16)
    far_lo = chip_swap(a2_lo)
    near_lo = core_swap(a2_lo)

    def last(own, near, far, s2):
        half = s2.shape[0]
        q0, q1, q2 = call(products2, (ch, own, near, far, core_swap(far), conv_weight), [s2.shape] * 3, half, mac * half)
        return shifted(q0, hop2), q1, shifted(q2, -hop2)

    far_hi, a2_lo = lax.optimization_barrier((far_hi, a2_lo))
    up_hi, q_hi, down_hi = last(a2_hi, near_hi, far_hi, s2_hi)
    far_lo, q_hi = lax.optimization_barrier((far_lo, q_hi))
    up_lo, q_lo, down_lo = last(a2_lo, near_lo, far_lo, s2_lo)
    out_hi = (f(s2_hi) + f(q_hi) + f(up_hi) + f(down_hi) + conv_bias[2]).astype(BF16)
    out_lo = (f(s2_lo) + f(q_lo) + f(up_lo) + f(down_lo) + conv_bias[2]).astype(BF16)
    return jnp.concatenate([out_lo, out_hi], axis=0)


def solution(mesh):
    return jax.shard_map(
        per_device,
        mesh=mesh,
        in_specs=(
            P("seq", "ch"),
            P(None, "ch"),
            P(None, "ch"),
            P(None, None, None, "ch"),
            P(None, "ch"),
        ),
        out_specs=P("seq", "ch"),
        check_vma=False,
    )
```

```python
import functools

import jax
import jax.numpy as jnp
from jax import lax
from jax.experimental import pallas as pl
from jax.experimental.pallas import tpu as pltpu
from jax.sharding import PartitionSpec as P

F32 = jnp.float32
BF16 = jnp.bfloat16
ERFC = (
    -1.26551223, 1.00002368, 0.37409196, 0.09678418, -0.18628806,
    0.27886807, -1.13520398, 1.48851587, -0.82215223, 0.17087277,
)
ROWS = 1024
MID = ROWS // 2
W = 384
R = 64
H = 416
N = H - 2 * R
A = MID - H + R
Q = N + R - A
M = 2 * A
X0 = 2 * N
X1 = M + 2 * R
REST = ROWS - 2 * H
SPAN = M + 2 * R
PART = 96
VMEM = pl.BlockSpec(memory_space=pltpu.VMEM)
SMEM = pl.BlockSpec(memory_space=pltpu.SMEM)
HBM = pl.BlockSpec(memory_space=pltpu.HBM)


def gelu(x):
    z = jnp.abs(x) * 0.7071067811865476
    t = 1.0 / (1.0 + 0.5 * z)
    poly = jnp.full_like(t, ERFC[-1])
    for c in ERFC[-2::-1]:
        poly = poly * t + c
    e = t * jnp.exp(poly - z * z)
    return 0.5 * x * jnp.where(x >= 0.0, 2.0 - e, e)


def shifted(array, by):
    size = lax.axis_size("seq")
    pairs = [(i, i + by) for i in range(size) if 0 <= i + by < size]
    return lax.ppermute(array, "seq", pairs)


def chip_swap(array):
    return lax.ppermute(array, "ch", [(i, i ^ 2) for i in range(4)])


def core_swap(array):
    return lax.ppermute(array, "ch", [(i, i ^ 1) for i in range(4)])


def dot(a, b):
    return jnp.dot(a, b, preferred_element_type=F32)


def wide(pieces, at, count):
    return jnp.concatenate([p[at : at + count, :] for p in pieces], axis=1)


def stage_kernel(ch_ref, w_hbm, o_ref, sems):
    copies = []
    for layer in range(3):
        for k in range(3):
            for p in range(4):
                row = pl.multiple_of((ch_ref[0] ^ p) * W, 128)
                copies.append(
                    pltpu.make_async_copy(
                        w_hbm.at[layer, k, pl.ds(row, W), :],
                        o_ref.at[layer, pl.ds(p * W, W), pl.ds(k * W, W)],
                        sems.at[len(copies)],
                    )
                )
    for copy in copies:
        copy.start()
    for copy in copies:
        copy.wait()


def finish(s, vec_ref, s_ref, a_ref, at, count):
    s = (s + vec_ref[0:1, :]).astype(BF16)
    s_ref[at : at + count, :] = s
    a_ref[at : at + count, :] = gelu(s.astype(F32) * vec_ref[1:2, :] + vec_ref[2:3, :]).astype(BF16)


def ends_kernel(p0, p1, p2, p3, bins_ref, vec_ref, w_ref, s_ref, a_ref):
    pieces = (p0, p1, p2, p3)
    for half in range(2):
        acc = dot(wide(pieces, half * H, N), w_ref[0, :, 0:W])
        acc += dot(wide(pieces, half * H + R, N), w_ref[0, :, W : 2 * W])
        acc += dot(wide(pieces, half * H + 2 * R, N), w_ref[0, :, 2 * W : 3 * W])
        at = R if half == 0 else ROWS - H + R
        finish(acc + bins_ref[at : at + N, :].astype(F32), vec_ref, s_ref, a_ref, half * N, N)


def middle_kernel(e0, e1, e2, e3, r0, r1, r2, r3, bins_ref, vec_ref, w_ref, s_ref, a_ref, buf):
    early, late = (e0, e1, e2, e3), (r0, r1, r2, r3)
    plan = (
        (late, REST, R), (early, 0, 2 * R),
        (early, H - 2 * R, 2 * R), (late, 0, REST), (early, H, 2 * R),
        (early, 2 * H - 2 * R, 2 * R), (late, REST + R, R),
    )
    to = 0
    for pieces, at, count in plan:
        for p, piece in enumerate(pieces):
            buf[to : to + count, p * W : (p + 1) * W] = piece[at : at + count, :]
        to += count
    second = 3 * R
    third = second + M + 2 * R
    acc = None
    for k in range(3):
        rows = [buf[k * R : k * R + R, :], buf[second + k * R : second + k * R + M, :], buf[third + k * R : third + k * R + R, :]]
        part = dot(jnp.concatenate(rows, axis=0), w_ref[0, :, k * W : (k + 1) * W])
        acc = part if acc is None else acc + part
    f = lambda at, count: bins_ref[at : at + count, :].astype(F32)
    acc += jnp.concatenate([f(0, R), f(H - R, M), f(ROWS - R, R)], axis=0)
    finish(acc, vec_ref, s_ref, a_ref, 0, X1)


def product_kernel(layer, p0, p1, p2, p3, w_ref, o0, o1, o2):
    full = dot(wide((p0, p1, p2, p3), 0, p0.shape[0]), w_ref[layer])
    for k, o in enumerate((o0, o1, o2)):
        o[...] = full[:, k * W : (k + 1) * W].astype(BF16)


def joined(vec_ref, s_ref, a_ref, at, count, *terms):
    total = None
    for ref, lo in terms:
        part = ref[lo : lo + count, :].astype(F32)
        total = part if total is None else total + part
    finish(total, vec_ref, s_ref, a_ref, at, count)


def join_early_kernel(s, q0, q1, q2, up, down, vec_ref, s_ref, a_ref):
    lo = N - Q
    joined(vec_ref, s_ref, a_ref, 0, Q, (s, lo), (q1, lo), (q2, N), (up, 0))
    joined(vec_ref, s_ref, a_ref, Q, Q, (s, N), (q1, N), (q0, lo), (down, lo))


def join_late_kernel(s0, t0, t1, t2, s1, u0, u1, u2, up0, down0, up1, down1, vec_ref, s_ref, a_ref):
    put = functools.partial(joined, vec_ref, s_ref, a_ref)
    b = A - R
    top = R + A
    put(0, R, (s1, 0), (u1, 0), (up1, 0), (u2, top))
    put(R, b, (s0, 0), (t1, 0), (up1, R), (u2, top + R))
    put(A, b, (s1, R), (u1, R), (up0, Q), (t2, N + Q))
    put(A + b, R, (s1, R + b), (u1, R + b), (up1, A), (u2, R + M))
    put(2 * A, R, (s1, top), (u1, top), (u0, 0), (down1, 0))
    put(2 * A + R, b, (s1, top + R), (u1, top + R), (t0, 0), (down0, 0))
    put(3 * A, b, (s0, N + Q), (t1, N + Q), (u0, R), (down1, R))
    put(3 * A + b, R, (s1, R + M), (u1, R + M), (u0, R + b), (down1, R + b))


def last_early_kernel(p0, p1, p2, p3, s_ref, vec_ref, w_ref, o_ref):
    pieces = (p0, p1, p2, p3)
    n = 2 * Q
    acc = dot(wide(pieces, 0, n), w_ref[2, :, W : 2 * W])
    acc += dot(wide(pieces, n, n), w_ref[2, :, 0:W])
    acc += dot(wide(pieces, 2 * n, n), w_ref[2, :, 2 * W : 3 * W])
    o_ref[...] = (s_ref[...].astype(F32) + acc + vec_ref[0:1, :]).astype(BF16)


def out_kernel(c, s, q, up0, up1, down0, down1, vec_ref, o_ref):
    def put(to, at, count):
        up, down, lo = (up0, down0, at) if at < M else (up1, down1, at - M)
        total = vec_ref[0:1, :]
        for ref, start in ((s, at), (q, at), (up, lo), (down, lo)):
            total = total + ref[start : start + count, :].astype(F32)
        o_ref[to : to + count, :] = total.astype(BF16)

    put(0, 0, A)
    o_ref[A : A + Q, :] = c[0:Q, :]
    put(A + Q, A, A)
    put(MID, M, A)
    o_ref[A + Q + M : A + 2 * Q + M, :] = c[Q : 2 * Q, :]
    put(ROWS - A, A + M, A)


def call(kernel, args, rows, flops=0, scratch=()):
    return pl.pallas_call(
        kernel,
        out_shape=[jax.ShapeDtypeStruct((r, W), BF16) for r in rows],
        in_specs=[VMEM] * len(args),
        out_specs=[VMEM] * len(rows),
        scratch_shapes=list(scratch),
        compiler_params=pltpu.CompilerParams(vmem_limit_bytes=20 * 1024 * 1024),
        cost_estimate=pl.CostEstimate(flops=flops, bytes_accessed=1024, transcendentals=0),
    )(*args)


def staged(ch, conv_weight):
    return pl.pallas_call(
        stage_kernel,
        out_shape=jax.ShapeDtypeStruct((3, 4 * W, 3 * W), BF16),
        in_specs=[SMEM, HBM],
        out_specs=VMEM,
        scratch_shapes=[pltpu.SemaphoreType.DMA((36,))],
        compiler_params=pltpu.CompilerParams(vmem_limit_bytes=40 * 1024 * 1024),
    )(ch, conv_weight)


def per_device(bins_in, pre_scale, pre_shift, conv_weight, conv_bias):
    after = lax.optimization_barrier
    ch = lax.axis_index("ch").astype(jnp.int32).reshape(1)
    hop1, hop2 = MID // 512, 4096 // ROWS
    mac = 2 * 4 * W * W * 3
    vec0 = jnp.stack([conv_bias[0], pre_scale[1], pre_shift[1]])
    vec1 = jnp.stack([conv_bias[1], pre_scale[2], pre_shift[2]])
    vec2 = conv_bias[2:3]

    def entry(x):
        return gelu(x.astype(F32) * pre_scale[0] + pre_shift[0]).astype(BF16)

    act_e = entry(jnp.concatenate([bins_in[:H], bins_in[ROWS - H :]], axis=0))
    far_e = chip_swap(act_e)
    low = shifted(act_e[-R:], 1)
    high = shifted(act_e[:R], -1)
    near_e = core_swap(act_e)
    weights = staged(ch, conv_weight)
    own_l = jnp.concatenate([entry(bins_in[H : ROWS - H]), low, high], axis=0)
    far_l = chip_swap(own_l)
    near_l = core_swap(own_l)
    far_e, weights = after((far_e, weights))
    g_e = (act_e, near_e, far_e, core_swap(far_e))

    s_x0, a_x0 = call(ends_kernel, (*g_e, bins_in, vec0, weights), [X0] * 2, mac * X0)
    far_x0 = chip_swap(a_x0)
    near_x0 = core_swap(a_x0)
    far_l, a_x0 = after((far_l, a_x0))
    g_l = (own_l, near_l, far_l, core_swap(far_l))
    s_x1, a_x1 = call(
        middle_kernel, (*g_e, *g_l, bins_in, vec0, weights), [X1] * 2, mac * X1,
        [pltpu.VMEM((8 * R + SPAN, 4 * W), BF16)],
    )
    far_x1 = chip_swap(a_x1)
    near_x1 = core_swap(a_x1)
    far_x0, a_x1 = after((far_x0, a_x1))
    g_x0 = (a_x0, near_x0, far_x0, core_swap(far_x0))
    t0, t1, t2 = call(functools.partial(product_kernel, 1), (*g_x0, weights), [X0] * 3, mac * X0)
    up0 = shifted(t0[N:], hop1)
    down0 = shifted(t2[:N], -hop1)
    far_x1, t1 = after((far_x1, t1))
    g_x1 = (a_x1, near_x1, far_x1, core_swap(far_x1))
    u0, u1, u2 = call(functools.partial(product_kernel, 1), (*g_x1, weights), [X1] * 3, mac * X1)
    up1 = shifted(u0[R + A :], hop1)
    down1 = shifted(u2[: R + A], -hop1)

    up0, down0, u1 = after((up0, down0, u1))
    s_c, a_c = call(join_early_kernel, (s_x0, t0, t1, t2, up0, down0, vec1), [2 * Q] * 2)
    low_c = [shifted(a_c[:PART], hop2), shifted(a_c[PART:], hop2)]
    high_c = [shifted(a_c[:PART], -hop2), shifted(a_c[PART:], -hop2)]
    up1, down1, low_c[0], high_c[0], a_c = after((up1, down1, low_c[0], high_c[0], a_c))
    s_d, a_d = call(
        join_late_kernel, (s_x0, t0, t1, t2, s_x1, u0, u1, u2, up0, down0, up1, down1, vec1), [2 * M] * 2
    )
    far_d = chip_swap(a_d)
    near_d = core_swap(a_d)
    far_d, low_c[1], high_c[1] = after((far_d, low_c[1], high_c[1]))
    own_c = jnp.concatenate([a_c, *low_c, *high_c], axis=0)
    far_c = chip_swap(own_c)
    near_c = core_swap(own_c)
    g_d = (a_d, near_d, far_d, core_swap(far_d))
    q0, q1, q2 = call(functools.partial(product_kernel, 2), (*g_d, weights), [2 * M] * 3, mac * 2 * M)
    up = [shifted(q0[:M], hop2), shifted(q0[M:], hop2)]
    down = [shifted(q2[:M], -hop2), shifted(q2[M:], -hop2)]
    far_c, up[0], down[0], q1 = after((far_c, up[0], down[0], q1))
    g_c = (own_c, near_c, far_c, core_swap(far_c))
    (out_c,) = call(last_early_kernel, (*g_c, s_c, vec2, weights), [2 * Q], mac * 2 * Q)
    up[1], down[1], out_c = after((up[1], down[1], out_c))
    (out,) = call(out_kernel, (out_c, s_d, q1, *up, *down, vec2), [ROWS])
    return out


def solution(mesh):
    return jax.shard_map(
        per_device,
        mesh=mesh,
        in_specs=(
            P("seq", "ch"),
            P(None, "ch"),
            P(None, "ch"),
            P(None, None, None, "ch"),
            P(None, "ch"),
        ),
        out_specs=P("seq", "ch"),
        check_vma=False,
    )
```

```python
import functools

import jax
import jax.numpy as jnp
from jax import lax
from jax.experimental import pallas as pl
from jax.experimental.pallas import tpu as pltpu
from jax.sharding import PartitionSpec as P

F32 = jnp.float32
BF16 = jnp.bfloat16
ERFC = (
    -1.26551223, 1.00002368, 0.37409196, 0.09678418, -0.18628806,
    0.27886807, -1.13520398, 1.48851587, -0.82215223, 0.17087277,
)
ROWS = 1024
MID = ROWS // 2
W = 384
R = 64
FIRST = MID - R
VMEM = pl.BlockSpec(memory_space=pltpu.VMEM)
SMEM = pl.BlockSpec(memory_space=pltpu.SMEM)
HBM = pl.BlockSpec(memory_space=pltpu.HBM)


def gelu(x):
    z = jnp.abs(x) * 0.7071067811865476
    t = 1.0 / (1.0 + 0.5 * z)
    poly = jnp.full_like(t, ERFC[-1])
    for c in ERFC[-2::-1]:
        poly = poly * t + c
    e = t * jnp.exp(poly - z * z)
    return 0.5 * x * jnp.where(x >= 0.0, 2.0 - e, e)


def shifted(array, by):
    size = lax.axis_size("seq")
    pairs = [(i, i + by) for i in range(size) if 0 <= i + by < size]
    return lax.ppermute(array, "seq", pairs)


def chip_swap(array):
    return lax.ppermute(array, "ch", [(i, i ^ 2) for i in range(4)])


def core_swap(array):
    return lax.ppermute(array, "ch", [(i, i ^ 1) for i in range(4)])


def dot(a, b):
    return jnp.dot(a, b, preferred_element_type=F32)


def stage_kernel(layer, ch_ref, w_hbm, o_ref, sems):
    copies = []
    for k in range(3):
        for p in range(4):
            row = pl.multiple_of((ch_ref[0] ^ p) * W, 128)
            copies.append(
                pltpu.make_async_copy(
                    w_hbm.at[layer, k, pl.ds(row, W), :],
                    o_ref.at[pl.ds(p * W, W), pl.ds(k * W, W)],
                    sems.at[len(copies)],
                )
            )
    for copy in copies:
        copy.start()
    for copy in copies:
        copy.wait()


def finish(total, vec_ref, s_ref, a_ref):
    s = (total + vec_ref[0:1, :]).astype(BF16)
    s_ref[...] = s
    a_ref[...] = gelu(s.astype(F32) * vec_ref[1:2, :] + vec_ref[2:3, :]).astype(BF16)


def near_kernel(plan, first_row, *refs):
    groups = max(g for g, _, _ in plan) + 1
    bins_ref, vec_ref, w_ref, s_ref, a_ref, buf = refs[4 * groups :]
    to = 0
    for g, at, count in plan:
        for p, piece in enumerate(refs[4 * g : 4 * g + 4]):
            buf[to : to + count, p * W : (p + 1) * W] = piece[at : at + count, :]
        to += count
    total = bins_ref[first_row : first_row + MID, :].astype(F32)
    for k in range(3):
        total = total + dot(buf[k * R : k * R + MID, :], w_ref[:, k * W : (k + 1) * W])
    finish(total, vec_ref, s_ref, a_ref)


def product_kernel(p0, p1, p2, p3, w_ref, o0, o1, o2):
    full = dot(jnp.concatenate([p[...] for p in (p0, p1, p2, p3)], axis=1), w_ref[...])
    for k, o in enumerate((o0, o1, o2)):
        o[...] = full[:, k * W : (k + 1) * W].astype(BF16)


def join_kernel(s0, t0, t1, t2, vec_ref, s_ref, a_ref):
    f = lambda ref: ref[...].astype(F32)
    finish(f(s0) + f(t0) + f(t1) + f(t2), vec_ref, s_ref, a_ref)


def out_kernel(s_lo, q_lo, up_lo, down_lo, s_hi, q_hi, up_hi, down_hi, vec_ref, o_ref):
    for to, refs in ((0, (s_lo, q_lo, up_lo, down_lo)), (MID, (s_hi, q_hi, up_hi, down_hi))):
        total = vec_ref[0:1, :]
        for ref in refs:
            total = total + ref[...].astype(F32)
        o_ref[to : to + MID, :] = total.astype(BF16)


def call(kernel, args, rows, scratch=()):
    return pl.pallas_call(
        kernel,
        out_shape=[jax.ShapeDtypeStruct((r, W), BF16) for r in rows],
        in_specs=[VMEM] * len(args),
        out_specs=[VMEM] * len(rows),
        scratch_shapes=list(scratch),
        compiler_params=pltpu.CompilerParams(vmem_limit_bytes=20 * 1024 * 1024),
        cost_estimate=pl.CostEstimate(flops=0, bytes_accessed=1024, transcendentals=0),
    )(*args)


def staged(layer, ch, conv_weight):
    return pl.pallas_call(
        functools.partial(stage_kernel, layer),
        out_shape=jax.ShapeDtypeStruct((4 * W, 3 * W), BF16),
        in_specs=[SMEM, HBM],
        out_specs=VMEM,
        scratch_shapes=[pltpu.SemaphoreType.DMA((12,))],
        compiler_params=pltpu.CompilerParams(vmem_limit_bytes=50 * 1024 * 1024),
    )(ch, conv_weight)


def per_device(bins_in, pre_scale, pre_shift, conv_weight, conv_bias):
    after = lax.optimization_barrier
    ch = lax.axis_index("ch").astype(jnp.int32).reshape(1)
    hop1, hop2 = 1, 4096 // ROWS
    vec0 = jnp.stack([conv_bias[0], pre_scale[1], pre_shift[1]])
    vec1 = jnp.stack([conv_bias[1], pre_scale[2], pre_shift[2]])
    vec2 = conv_bias[2:3]
    halves = [MID] * 3
    scratch = [pltpu.VMEM((MID + 2 * R, 4 * W), BF16)]

    def entry(x):
        return gelu(x.astype(F32) * pre_scale[0] + pre_shift[0]).astype(BF16)

    act_1 = entry(bins_in[FIRST:])
    far_1 = chip_swap(act_1)
    near_1 = core_swap(act_1)
    act_3 = entry(bins_in[:FIRST])
    low = shifted(act_1[-R:], 1)
    high = shifted(act_3[:R], -1)
    w0 = staged(0, ch, conv_weight)
    act_2 = jnp.concatenate([low, high], axis=0)
    far_2 = chip_swap(act_2)
    near_2 = core_swap(act_2)
    far_3 = chip_swap(act_3)
    near_3 = core_swap(act_3)
    far_1, far_2, near_2, w0 = after((far_1, far_2, near_2, w0))
    g_1 = (act_1, near_1, far_1, core_swap(far_1))
    g_2 = (act_2, near_2, far_2, core_swap(far_2))
    plan_hi = ((0, 0, ROWS - FIRST), (1, R, R))
    s_hi, a_hi = call(
        functools.partial(near_kernel, plan_hi, MID), (*g_1, *g_2, bins_in, vec0, w0), halves[:2], scratch
    )
    far_hi = chip_swap(a_hi)
    near_hi = core_swap(a_hi)
    far_3, a_hi = after((far_3, a_hi))
    g_3 = (act_3, near_3, far_3, core_swap(far_3))
    plan_lo = ((1, 0, R), (2, 0, FIRST), (0, 0, 2 * R))
    s_lo, a_lo = call(
        functools.partial(near_kernel, plan_lo, 0), (*g_1, *g_2, *g_3, bins_in, vec0, w0), halves[:2], scratch
    )
    far_lo = chip_swap(a_lo)
    near_lo = core_swap(a_lo)

    ch, a_lo = after((ch, a_lo))
    w1 = staged(1, ch, conv_weight)
    far_hi, near_lo, w1 = after((far_hi, near_lo, w1))
    t0, t1, t2 = call(product_kernel, (a_hi, near_hi, far_hi, core_swap(far_hi), w1), halves)
    up = shifted(t0, hop1)
    far_lo, t1 = after((far_lo, t1))
    u0, u1, u2 = call(product_kernel, (a_lo, near_lo, far_lo, core_swap(far_lo), w1), halves)
    down = shifted(u2, -hop1)
    s_lo, a_lo = call(join_kernel, (s_lo, u1, up, t2, vec1), halves[:2])
    far_lo = chip_swap(a_lo)
    near_lo = core_swap(a_lo)
    ch, a_lo = after((ch, a_lo))
    w2 = staged(2, ch, conv_weight)
    down, w2 = after((down, w2))
    s_hi, a_hi = call(join_kernel, (s_hi, t1, u0, down, vec1), halves[:2])
    far_hi = chip_swap(a_hi)
    near_hi = core_swap(a_hi)

    def last(own, near, far):
        q0, q1, q2 = call(product_kernel, (own, near, far, core_swap(far), w2), halves)
        return q1, shifted(q0, hop2), shifted(q2, -hop2)

    far_lo, a_hi = after((far_lo, a_hi))
    q_lo, up_lo, down_lo = last(a_lo, near_lo, far_lo)
    far_hi, q_lo = after((far_hi, q_lo))
    q_hi, up_hi, down_hi = last(a_hi, near_hi, far_hi)
    (out,) = call(out_kernel, (s_lo, q_lo, up_lo, down_lo, s_hi, q_hi, up_hi, down_hi, vec2), [ROWS])
    return out


def solution(mesh):
    return jax.shard_map(
        per_device,
        mesh=mesh,
        in_specs=(
            P("seq", "ch"),
            P(None, "ch"),
            P(None, "ch"),
            P(None, None, None, "ch"),
            P(None, "ch"),
        ),
        out_specs=P("seq", "ch"),
        check_vma=False,
    )
```

```python
import functools

import jax
import jax.numpy as jnp
from jax import lax
from jax.experimental import pallas as pl
from jax.experimental.pallas import tpu as pltpu
from jax.sharding import PartitionSpec as P

F32 = jnp.float32
BF16 = jnp.bfloat16
ERFC = (
    -1.26551223, 1.00002368, 0.37409196, 0.09678418, -0.18628806,
    0.27886807, -1.13520398, 1.48851587, -0.82215223, 0.17087277,
)
ROWS = 1024
MID = ROWS // 2
W = 384
R = 64
FIRST = MID - R
VMEM = pl.BlockSpec(memory_space=pltpu.VMEM)
SMEM = pl.BlockSpec(memory_space=pltpu.SMEM)
HBM = pl.BlockSpec(memory_space=pltpu.HBM)


def gelu(x):
    z = jnp.abs(x) * 0.7071067811865476
    t = 1.0 / (1.0 + 0.5 * z)
    poly = jnp.full_like(t, ERFC[-1])
    for c in ERFC[-2::-1]:
        poly = poly * t + c
    e = t * jnp.exp(poly - z * z)
    return 0.5 * x * jnp.where(x >= 0.0, 2.0 - e, e)


def shifted(array, by):
    size = lax.axis_size("seq")
    pairs = [(i, i + by) for i in range(size) if 0 <= i + by < size]
    return lax.ppermute(array, "seq", pairs)


def chip_swap(array):
    return lax.ppermute(array, "ch", [(i, i ^ 2) for i in range(4)])


def core_swap(array):
    return lax.ppermute(array, "ch", [(i, i ^ 1) for i in range(4)])


def core_swaps(array, parts):
    n = array.shape[0] // parts
    return [core_swap(array[i * n : i * n + n]) for i in range(parts)]


def dot(a, b):
    return jnp.dot(a, b, preferred_element_type=F32)


def stage_kernel(layer, ch_ref, w_hbm, o_ref, sems):
    copies = []
    for k in range(3):
        for p in range(4):
            row = pl.multiple_of((ch_ref[0] ^ p) * W, 128)
            copies.append(
                pltpu.make_async_copy(
                    w_hbm.at[layer, k, pl.ds(row, W), :],
                    o_ref.at[pl.ds(p * W, W), pl.ds(k * W, W)],
                    sems.at[len(copies)],
                )
            )
    for copy in copies:
        copy.start()
    for copy in copies:
        copy.wait()


def finish(total, vec_ref, s_ref, a_ref):
    s = (total + vec_ref[0:1, :]).astype(BF16)
    s_ref[...] = s
    a_ref[...] = gelu(s.astype(F32) * vec_ref[1:2, :] + vec_ref[2:3, :]).astype(BF16)


def near_kernel(plan, first_row, *refs):
    groups = max(g for g, _, _ in plan) + 1
    bins_ref, vec_ref, w_ref, s_ref, a_ref, buf = refs[4 * groups :]
    to = 0
    for g, at, count in plan:
        for p, piece in enumerate(refs[4 * g : 4 * g + 4]):
            buf[to : to + count, p * W : (p + 1) * W] = piece[at : at + count, :]
        to += count
    total = bins_ref[first_row : first_row + MID, :].astype(F32)
    for k in range(3):
        total = total + dot(buf[k * R : k * R + MID, :], w_ref[:, k * W : (k + 1) * W])
    finish(total, vec_ref, s_ref, a_ref)


def product_kernel(*refs):
    pieces, (w_ref, o0, o1, o2) = refs[:-4], refs[-4:]
    near_far = jnp.concatenate([p[...] for p in pieces[3:]], axis=0)
    full = dot(jnp.concatenate([p[...] for p in pieces[:3]] + [near_far], axis=1), w_ref[...])
    for k, o in enumerate((o0, o1, o2)):
        o[...] = full[:, k * W : (k + 1) * W].astype(BF16)


def join_kernel(s0, t0, t1, t2, vec_ref, s_ref, a_ref):
    f = lambda ref: ref[...].astype(F32)
    finish(f(s0) + f(t0) + f(t1) + f(t2), vec_ref, s_ref, a_ref)


def out_kernel(s_lo, q_lo, up_lo, down_lo, s_hi, q_hi, up_hi, down_hi, vec_ref, o_ref):
    for to, refs in ((0, (s_lo, q_lo, up_lo, down_lo)), (MID, (s_hi, q_hi, up_hi, down_hi))):
        total = vec_ref[0:1, :]
        for ref in refs:
            total = total + ref[...].astype(F32)
        o_ref[to : to + MID, :] = total.astype(BF16)


def call(kernel, args, rows, scratch=()):
    return pl.pallas_call(
        kernel,
        out_shape=[jax.ShapeDtypeStruct((r, W), BF16) for r in rows],
        in_specs=[VMEM] * len(args),
        out_specs=[VMEM] * len(rows),
        scratch_shapes=list(scratch),
        compiler_params=pltpu.CompilerParams(vmem_limit_bytes=20 * 1024 * 1024),
        cost_estimate=pl.CostEstimate(flops=0, bytes_accessed=1024, transcendentals=0),
    )(*args)


def staged(layer, ch, conv_weight):
    return pl.pallas_call(
        functools.partial(stage_kernel, layer),
        out_shape=jax.ShapeDtypeStruct((4 * W, 3 * W), BF16),
        in_specs=[SMEM, HBM],
        out_specs=VMEM,
        scratch_shapes=[pltpu.SemaphoreType.DMA((12,))],
        compiler_params=pltpu.CompilerParams(vmem_limit_bytes=50 * 1024 * 1024),
    )(ch, conv_weight)


def per_device(bins_in, pre_scale, pre_shift, conv_weight, conv_bias):
    after = lax.optimization_barrier
    ch = lax.axis_index("ch").astype(jnp.int32).reshape(1)
    hop1, hop2 = 1, 4096 // ROWS
    vec0 = jnp.stack([conv_bias[0], pre_scale[1], pre_shift[1]])
    vec1 = jnp.stack([conv_bias[1], pre_scale[2], pre_shift[2]])
    vec2 = conv_bias[2:3]
    halves = [MID] * 3
    scratch = [pltpu.VMEM((MID + 2 * R, 4 * W), BF16)]

    def entry(x):
        return gelu(x.astype(F32) * pre_scale[0] + pre_shift[0]).astype(BF16)

    act_1 = entry(bins_in[FIRST:])
    far_1 = chip_swap(act_1)
    near_1 = core_swap(act_1)
    act_3 = entry(bins_in[:FIRST])
    low = shifted(act_1[-R:], 1)
    high = shifted(act_3[:R], -1)
    w0 = staged(0, ch, conv_weight)
    act_2 = jnp.concatenate([low, high], axis=0)
    far_2 = chip_swap(act_2)
    near_2 = core_swap(act_2)
    far_3 = chip_swap(act_3)
    near_3 = core_swap(act_3)
    far_1, far_2, far_3, w0 = after((far_1, far_2, far_3, w0))
    g_1 = (act_1, near_1, far_1, core_swap(far_1))
    g_2 = (act_2, near_2, far_2, core_swap(far_2))
    plan_hi = ((0, 0, ROWS - FIRST), (1, R, R))
    s_hi, a_hi = call(
        functools.partial(near_kernel, plan_hi, MID), (*g_1, *g_2, bins_in, vec0, w0), halves[:2], scratch
    )
    far_hi = chip_swap(a_hi)
    near_hi = core_swap(a_hi)
    near_3, a_hi = after((near_3, a_hi))
    g_3 = (act_3, near_3, far_3, core_swap(far_3))
    plan_lo = ((1, 0, R), (2, 0, FIRST), (0, 0, 2 * R))
    s_lo, a_lo = call(
        functools.partial(near_kernel, plan_lo, 0), (*g_1, *g_2, *g_3, bins_in, vec0, w0), halves[:2], scratch
    )
    far_lo = chip_swap(a_lo)
    near_lo = core_swap(a_lo)

    ch, a_lo = after((ch, a_lo))
    w1 = staged(1, ch, conv_weight)
    far_hi, w1 = after((far_hi, w1))
    t0, t1, t2 = call(product_kernel, (a_hi, near_hi, far_hi, *core_swaps(far_hi, 2), w1), halves)
    up = shifted(t0, hop1)
    far_lo, t1 = after((far_lo, t1))
    u0, u1, u2 = call(product_kernel, (a_lo, near_lo, far_lo, *core_swaps(far_lo, 2), w1), halves)
    down = shifted(u2, -hop1)
    s_lo, a_lo = call(join_kernel, (s_lo, u1, up, t2, vec1), halves[:2])
    far_lo = chip_swap(a_lo)
    near_lo = core_swap(a_lo)
    ch, a_lo = after((ch, a_lo))
    w2 = staged(2, ch, conv_weight)
    down, w2 = after((down, w2))
    s_hi, a_hi = call(join_kernel, (s_hi, t1, u0, down, vec1), halves[:2])
    far_hi = chip_swap(a_hi)
    near_hi = core_swap(a_hi)

    def last(own, near, far, parts):
        q0, q1, q2 = call(product_kernel, (own, near, far, *core_swaps(far, parts), w2), halves)
        return q1, shifted(q0, hop2), shifted(q2, -hop2)

    far_lo, a_hi = after((far_lo, a_hi))
    q_lo, up_lo, down_lo = last(a_lo, near_lo, far_lo, 2)
    far_hi, q_lo = after((far_hi, q_lo))
    q_hi, up_hi, down_hi = last(a_hi, near_hi, far_hi, 2)
    (out,) = call(out_kernel, (s_lo, q_lo, up_lo, down_lo, s_hi, q_hi, up_hi, down_hi, vec2), [ROWS])
    return out


def solution(mesh):
    return jax.shard_map(
        per_device,
        mesh=mesh,
        in_specs=(
            P("seq", "ch"),
            P(None, "ch"),
            P(None, "ch"),
            P(None, None, None, "ch"),
            P(None, "ch"),
        ),
        out_specs=P("seq", "ch"),
        check_vma=False,
    )
```

```python
import functools

import jax
import jax.numpy as jnp
from jax import lax
from jax.experimental import pallas as pl
from jax.experimental.pallas import tpu as pltpu
from jax.sharding import PartitionSpec as P

F32 = jnp.float32
BF16 = jnp.bfloat16
ERFC = (
    -1.26551223, 1.00002368, 0.37409196, 0.09678418, -0.18628806,
    0.27886807, -1.13520398, 1.48851587, -0.82215223, 0.17087277,
)
ROWS = 1024
MID = ROWS // 2
W = 384
R = 64
FIRST = MID - R
COST = 10**10
VMEM = pl.BlockSpec(memory_space=pltpu.VMEM)
SMEM = pl.BlockSpec(memory_space=pltpu.SMEM)
HBM = pl.BlockSpec(memory_space=pltpu.HBM)


def gelu(x):
    z = jnp.abs(x) * 0.7071067811865476
    t = 1.0 / (1.0 + 0.5 * z)
    poly = jnp.full_like(t, ERFC[-1])
    for c in ERFC[-2::-1]:
        poly = poly * t + c
    e = t * jnp.exp(poly - z * z)
    return 0.5 * x * jnp.where(x >= 0.0, 2.0 - e, e)


def shifted(array, by):
    size = lax.axis_size("seq")
    pairs = [(i, i + by) for i in range(size) if 0 <= i + by < size]
    return lax.ppermute(array, "seq", pairs)


def chip_swap(array):
    return lax.ppermute(array, "ch", [(i, i ^ 2) for i in range(4)])


def core_swap(array):
    return lax.ppermute(array, "ch", [(i, i ^ 1) for i in range(4)])


def core_swaps(array, parts):
    n = array.shape[0] // parts
    return [core_swap(array[i * n : i * n + n]) for i in range(parts)]


def dot(a, b):
    return jnp.dot(a, b, preferred_element_type=F32)


def stage_kernel(layer, ch_ref, w_hbm, o_ref, sems):
    copies = []
    for k in range(3):
        for p in range(4):
            row = pl.multiple_of((ch_ref[0] ^ p) * W, 128)
            copies.append(
                pltpu.make_async_copy(
                    w_hbm.at[layer, k, pl.ds(row, W), :],
                    o_ref.at[pl.ds(p * W, W), pl.ds(k * W, W)],
                    sems.at[len(copies)],
                )
            )
    for copy in copies:
        copy.start()
    for copy in copies:
        copy.wait()


def finish(total, vec_ref, s_ref, a_ref):
    s = (total + vec_ref[0:1, :]).astype(BF16)
    s_ref[...] = s
    a_ref[...] = gelu(s.astype(F32) * vec_ref[1:2, :] + vec_ref[2:3, :]).astype(BF16)


def near_kernel(plan, first_row, *refs):
    groups = max(g for g, _, _ in plan) + 1
    bins_ref, vec_ref, w_ref, s_ref, a_ref, buf = refs[4 * groups :]
    to = 0
    for g, at, count in plan:
        for p, piece in enumerate(refs[4 * g : 4 * g + 4]):
            buf[to : to + count, p * W : (p + 1) * W] = piece[at : at + count, :]
        to += count
    total = bins_ref[first_row : first_row + MID, :].astype(F32)
    for k in range(3):
        total = total + dot(buf[k * R : k * R + MID, :], w_ref[:, k * W : (k + 1) * W])
    finish(total, vec_ref, s_ref, a_ref)


def product_kernel(*refs):
    pieces, (w_ref, o0, o1, o2) = refs[:-4], refs[-4:]
    full = dot(joined(pieces), w_ref[...])
    for k, o in enumerate((o0, o1, o2)):
        o[...] = full[:, k * W : (k + 1) * W].astype(BF16)


def join_kernel(s0, t0, t1, t2, vec_ref, s_ref, a_ref):
    f = lambda ref: ref[...].astype(F32)
    finish(f(s0) + f(t0) + f(t1) + f(t2), vec_ref, s_ref, a_ref)


def joined(refs, fars=1):
    far = jnp.concatenate([p[...] for p in refs[2 : 2 + fars]], axis=0)
    near_far = jnp.concatenate([p[...] for p in refs[2 + fars :]], axis=0)
    return jnp.concatenate([refs[0][...], refs[1][...], far, near_far], axis=1)


def part_kernel(*refs):
    own, low, (s_ref, vec_ref, w_ref, o_ref) = refs[:4], refs[4:8], refs[8:]
    total = s_ref[...].astype(F32) + vec_ref[0:1, :]
    total = total + dot(joined(own, 1), w_ref[:, W : 2 * W])
    o_ref[...] = total + dot(joined(low, 1), w_ref[:, 0:W])


def upper_kernel(s_hi, q_hi, up_hi, down_hi, vec_ref, o_ref):
    total = vec_ref[0:1, :]
    for ref in (s_hi, q_hi, up_hi, down_hi):
        total = total + ref[...].astype(F32)
    o_ref[...] = total.astype(BF16)


def out_kernel(*refs):
    high, (part, upper, w_ref, o_ref) = refs[:4], refs[4:]
    o_ref[:MID, :] = (part[...] + dot(joined(high), w_ref[:, 2 * W : 3 * W])).astype(BF16)
    o_ref[MID:, :] = upper[...]


def call(kernel, args, rows, scratch=(), dtype=BF16, flops=0):
    return pl.pallas_call(
        kernel,
        out_shape=[jax.ShapeDtypeStruct((r, W), dtype) for r in rows],
        in_specs=[VMEM] * len(args),
        out_specs=[VMEM] * len(rows),
        scratch_shapes=list(scratch),
        compiler_params=pltpu.CompilerParams(vmem_limit_bytes=20 * 1024 * 1024),
        cost_estimate=pl.CostEstimate(flops=flops, bytes_accessed=1024, transcendentals=0),
    )(*args)


def staged(layer, ch, conv_weight):
    return pl.pallas_call(
        functools.partial(stage_kernel, layer),
        out_shape=jax.ShapeDtypeStruct((4 * W, 3 * W), BF16),
        in_specs=[SMEM, HBM],
        out_specs=VMEM,
        scratch_shapes=[pltpu.SemaphoreType.DMA((12,))],
        compiler_params=pltpu.CompilerParams(vmem_limit_bytes=50 * 1024 * 1024),
    )(ch, conv_weight)


def per_device(bins_in, pre_scale, pre_shift, conv_weight, conv_bias):
    after = lax.optimization_barrier
    ch = lax.axis_index("ch").astype(jnp.int32).reshape(1)
    hop1, hop2 = 1, 4096 // ROWS
    vec0 = jnp.stack([conv_bias[0], pre_scale[1], pre_shift[1]])
    vec1 = jnp.stack([conv_bias[1], pre_scale[2], pre_shift[2]])
    vec2 = conv_bias[2:3]
    halves = [MID] * 3
    scratch = [pltpu.VMEM((MID + 2 * R, 4 * W), BF16)]

    def entry(x):
        return gelu(x.astype(F32) * pre_scale[0] + pre_shift[0]).astype(BF16)

    act_1 = entry(bins_in[FIRST:])
    far_1 = chip_swap(act_1)
    near_1 = core_swap(act_1)
    act_3 = entry(bins_in[:FIRST])
    low = shifted(act_1[-R:], 1)
    high = shifted(act_3[:R], -1)
    low, act_3 = after((low, act_3))
    w0 = staged(0, ch, conv_weight)
    act_2 = jnp.concatenate([low, high], axis=0)
    far_2 = chip_swap(act_2)
    near_2 = core_swap(act_2)
    far_3 = chip_swap(act_3)
    near_3 = core_swap(act_3)
    far_1, far_2, far_3, w0 = after((far_1, far_2, far_3, w0))
    g_1 = (act_1, near_1, far_1, core_swap(far_1))
    g_2 = (act_2, near_2, far_2, core_swap(far_2))
    plan_hi = ((0, 0, ROWS - FIRST), (1, R, R))
    s_hi, a_hi = call(
        functools.partial(near_kernel, plan_hi, MID), (*g_1, *g_2, bins_in, vec0, w0), halves[:2], scratch
    )
    far_hi = chip_swap(a_hi)
    near_hi = core_swap(a_hi)
    near_3, a_hi = after((near_3, a_hi))
    g_3 = (act_3, near_3, far_3, core_swap(far_3))
    plan_lo = ((1, 0, R), (2, 0, FIRST), (0, 0, 2 * R))
    s_lo, a_lo = call(
        functools.partial(near_kernel, plan_lo, 0), (*g_1, *g_2, *g_3, bins_in, vec0, w0), halves[:2], scratch
    )
    far_lo = chip_swap(a_lo)
    near_lo = core_swap(a_lo)

    ch, a_lo = after((ch, a_lo))
    w1 = staged(1, ch, conv_weight)
    far_hi, w1 = after((far_hi, w1))
    t0, t1, t2 = call(product_kernel, (a_hi, near_hi, far_hi, *core_swaps(far_hi, 2), w1), halves)
    up = shifted(t0, hop1)
    far_lo, t1 = after((far_lo, t1))
    u0, u1, u2 = call(product_kernel, (a_lo, near_lo, far_lo, *core_swaps(far_lo, 2), w1), halves)
    down = shifted(u2, -hop1)
    s_lo, a_lo = call(join_kernel, (s_lo, u1, up, t2, vec1), halves[:2])
    from_low = shifted(a_lo, hop2)
    from_high = shifted(a_lo, -hop2)
    ch, a_lo = after((ch, a_lo))
    w2 = staged(2, ch, conv_weight)
    s_hi, a_hi = call(join_kernel, (s_hi, t1, u0, down, vec1), halves[:2])
    far_hi = chip_swap(a_hi)
    near_hi = core_swap(a_hi)
    far_hi, from_low, from_high, w2 = after((far_hi, from_low, from_high, w2))
    a_lo, a_hi = after((a_lo, a_hi))

    far_own = chip_swap(a_lo)
    near_own = core_swap(a_lo)
    near_low = core_swap(from_low)
    near_high = core_swap(from_high)
    g_hi = [a_hi, near_hi, far_hi, *core_swaps(far_hi, 2)]
    *g_hi, far_own, near_own, near_low, near_high = after((*g_hi, far_own, near_own, near_low, near_high))
    q0, q_hi, q2 = call(product_kernel, (*g_hi, w2), halves)
    up_hi = shifted(q0, hop2)
    down_hi = shifted(q2, -hop2)
    from_low, from_high, far_own, q_hi = after((from_low, from_high, far_own, q_hi))
    far_low = chip_swap(from_low)
    far_high = chip_swap(from_high)
    g_own = (a_lo, near_own, far_own, core_swap(far_own))
    g_low = (from_low, near_low, far_low, core_swap(far_low))
    g_high = (from_high, near_high, far_high, core_swap(far_high))
    (part,) = call(part_kernel, (*g_own, *g_low, s_lo, vec2, w2), halves[:1], dtype=F32)
    up_hi, down_hi, part = after((up_hi, down_hi, part))
    (upper,) = call(upper_kernel, (s_hi, q_hi, up_hi, down_hi, vec2), halves[:1], flops=COST)
    (out,) = call(out_kernel, (*g_high, part, upper, w2), [ROWS])
    return out


def solution(mesh):
    return jax.shard_map(
        per_device,
        mesh=mesh,
        in_specs=(
            P("seq", "ch"),
            P(None, "ch"),
            P(None, "ch"),
            P(None, None, None, "ch"),
            P(None, "ch"),
        ),
        out_specs=P("seq", "ch"),
        check_vma=False,
    )
```

```python
import functools

import jax
import jax.numpy as jnp
from jax import lax
from jax.experimental import pallas as pl
from jax.experimental.pallas import tpu as pltpu
from jax.sharding import PartitionSpec as P

F32 = jnp.float32
BF16 = jnp.bfloat16
ERFC = (
    -1.26551223, 1.00002368, 0.37409196, 0.09678418, -0.18628806,
    0.27886807, -1.13520398, 1.48851587, -0.82215223, 0.17087277,
)
ROWS = 1024
MID = ROWS // 2
W = 384
R = 64
FIRST = MID - R
COST = 10**10
VMEM = pl.BlockSpec(memory_space=pltpu.VMEM)
SMEM = pl.BlockSpec(memory_space=pltpu.SMEM)
HBM = pl.BlockSpec(memory_space=pltpu.HBM)


def gelu(x):
    z = jnp.abs(x) * 0.7071067811865476
    t = 1.0 / (1.0 + 0.5 * z)
    poly = jnp.full_like(t, ERFC[-1])
    for c in ERFC[-2::-1]:
        poly = poly * t + c
    e = t * jnp.exp(poly - z * z)
    return 0.5 * x * jnp.where(x >= 0.0, 2.0 - e, e)


def shifted(array, by):
    size = lax.axis_size("seq")
    pairs = [(i, i + by) for i in range(size) if 0 <= i + by < size]
    return lax.ppermute(array, "seq", pairs)


def chip_swap(array):
    return lax.ppermute(array, "ch", [(i, i ^ 2) for i in range(4)])


def core_swap(array):
    return lax.ppermute(array, "ch", [(i, i ^ 1) for i in range(4)])


def core_swaps(array, parts):
    n = array.shape[0] // parts
    return [core_swap(array[i * n : i * n + n]) for i in range(parts)]


def dot(a, b):
    return jnp.dot(a, b, preferred_element_type=F32)


def stage_kernel(layer, ch_ref, w_hbm, o_ref, sems):
    copies = []
    for k in range(3):
        for p in range(4):
            row = pl.multiple_of((ch_ref[0] ^ p) * W, 128)
            copies.append(
                pltpu.make_async_copy(
                    w_hbm.at[layer, k, pl.ds(row, W), :],
                    o_ref.at[pl.ds(p * W, W), pl.ds(k * W, W)],
                    sems.at[len(copies)],
                )
            )
    for copy in copies:
        copy.start()
    for copy in copies:
        copy.wait()


def finish(total, vec_ref, s_ref, a_ref):
    s = (total + vec_ref[0:1, :]).astype(BF16)
    s_ref[...] = s
    a_ref[...] = gelu(s.astype(F32) * vec_ref[1:2, :] + vec_ref[2:3, :]).astype(BF16)


def near_kernel(plan, parts, first_row, *refs):
    groups, at = [], 0
    for part in parts:
        group = refs[at : at + 3 + part]
        groups.append([[group[0]], [group[1]], [group[2]], group[3:]])
        at += 3 + part
    bins_ref, vec_ref, w_ref, s_ref, a_ref, buf = refs[at:]
    to = 0
    for g, at, count in plan:
        for p, pieces in enumerate(groups[g]):
            low = 0
            for piece in pieces:
                start, stop = max(at, low), min(at + count, low + piece.shape[0])
                if start < stop:
                    buf[to + start - at : to + stop - at, p * W : (p + 1) * W] = piece[start - low : stop - low, :]
                low += piece.shape[0]
        to += count
    total = bins_ref[first_row : first_row + MID, :].astype(F32)
    for k in range(3):
        total = total + dot(buf[k * R : k * R + MID, :], w_ref[:, k * W : (k + 1) * W])
    finish(total, vec_ref, s_ref, a_ref)


def product_kernel(*refs):
    pieces, (w_ref, o0, o1, o2) = refs[:-4], refs[-4:]
    full = dot(joined(pieces), w_ref[...])
    for k, o in enumerate((o0, o1, o2)):
        o[...] = full[:, k * W : (k + 1) * W].astype(BF16)


def join_kernel(s0, t0, t1, t2, vec_ref, s_ref, a_ref):
    f = lambda ref: ref[...].astype(F32)
    finish(f(s0) + f(t0) + f(t1) + f(t2), vec_ref, s_ref, a_ref)


def joined(refs, fars=1):
    far = jnp.concatenate([p[...] for p in refs[2 : 2 + fars]], axis=0)
    near_far = jnp.concatenate([p[...] for p in refs[2 + fars :]], axis=0)
    return jnp.concatenate([refs[0][...], refs[1][...], far, near_far], axis=1)


def rims_kernel(low_ref, high_ref, o_ref):
    o_ref[:R, :] = low_ref[...]
    o_ref[R:, :] = high_ref[...]


def part_kernel(*refs):
    own, low, (s_ref, vec_ref, w_ref, o_ref) = refs[:4], refs[4:8], refs[8:]
    total = s_ref[...].astype(F32) + vec_ref[0:1, :]
    total = total + dot(joined(own, 1), w_ref[:, W : 2 * W])
    o_ref[...] = total + dot(joined(low, 1), w_ref[:, 0:W])


def upper_kernel(s_hi, q_hi, up_hi, down_hi, vec_ref, o_ref):
    total = vec_ref[0:1, :]
    for ref in (s_hi, q_hi, up_hi, down_hi):
        total = total + ref[...].astype(F32)
    o_ref[...] = total.astype(BF16)


def out_kernel(*refs):
    high, (part, upper, w_ref, o_ref) = refs[:4], refs[4:]
    o_ref[:MID, :] = (part[...] + dot(joined(high), w_ref[:, 2 * W : 3 * W])).astype(BF16)
    o_ref[MID:, :] = upper[...]


def call(kernel, args, rows, scratch=(), dtype=BF16, flops=0):
    return pl.pallas_call(
        kernel,
        out_shape=[jax.ShapeDtypeStruct((r, W), dtype) for r in rows],
        in_specs=[VMEM] * len(args),
        out_specs=[VMEM] * len(rows),
        scratch_shapes=list(scratch),
        compiler_params=pltpu.CompilerParams(vmem_limit_bytes=20 * 1024 * 1024),
        cost_estimate=pl.CostEstimate(flops=flops, bytes_accessed=1024, transcendentals=0),
    )(*args)


def staged(layer, ch, conv_weight):
    return pl.pallas_call(
        functools.partial(stage_kernel, layer),
        out_shape=jax.ShapeDtypeStruct((4 * W, 3 * W), BF16),
        in_specs=[SMEM, HBM],
        out_specs=VMEM,
        scratch_shapes=[pltpu.SemaphoreType.DMA((12,))],
        compiler_params=pltpu.CompilerParams(vmem_limit_bytes=50 * 1024 * 1024),
    )(ch, conv_weight)


def per_device(bins_in, pre_scale, pre_shift, conv_weight, conv_bias):
    after = lax.optimization_barrier
    ch = lax.axis_index("ch").astype(jnp.int32).reshape(1)
    hop1, hop2 = 1, 4096 // ROWS
    vec0 = jnp.stack([conv_bias[0], pre_scale[1], pre_shift[1]])
    vec1 = jnp.stack([conv_bias[1], pre_scale[2], pre_shift[2]])
    vec2 = conv_bias[2:3]
    halves = [MID] * 3
    scratch = [pltpu.VMEM((MID + 2 * R, 4 * W), BF16)]

    def entry(x):
        return gelu(x.astype(F32) * pre_scale[0] + pre_shift[0]).astype(BF16)

    act_1 = entry(bins_in[FIRST:])
    far_1 = chip_swap(act_1)
    near_1 = core_swap(act_1)
    act_3 = entry(bins_in[:FIRST])
    low = shifted(act_1[-R:], 1)
    high = shifted(act_3[:R], -1)
    w0 = staged(0, ch, conv_weight)
    low, high, w0 = after((low, high, w0))
    (act_2,) = call(rims_kernel, (low, high), [2 * R])
    act_2, act_3 = after((act_2, act_3))
    far_2 = chip_swap(act_2)
    near_2 = core_swap(act_2)
    far_3 = chip_swap(act_3)
    near_3 = core_swap(act_3)
    far_1, far_2, near_1 = after((far_1, far_2, near_1))
    g_1 = (act_1, near_1, far_1, *core_swaps(far_1, 2))
    g_2 = (act_2, near_2, far_2, core_swap(far_2))
    g_1, g_2, far_3 = after((g_1, g_2, far_3))
    plan_hi = ((0, 0, ROWS - FIRST), (1, R, R))
    s_hi, a_hi = call(
        functools.partial(near_kernel, plan_hi, (2, 1), MID), (*g_1, *g_2, bins_in, vec0, w0), halves[:2], scratch
    )
    far_hi = chip_swap(a_hi)
    near_hi = core_swap(a_hi)
    near_3, a_hi = after((near_3, a_hi))
    g_3 = (act_3, near_3, far_3, core_swap(far_3))
    plan_lo = ((1, 0, R), (2, 0, FIRST), (0, 0, 2 * R))
    s_lo, a_lo = call(
        functools.partial(near_kernel, plan_lo, (2, 1, 1), 0), (*g_1, *g_2, *g_3, bins_in, vec0, w0), halves[:2], scratch
    )
    far_lo = chip_swap(a_lo)
    near_lo = core_swap(a_lo)

    ch, a_lo = after((ch, a_lo))
    w1 = staged(1, ch, conv_weight)
    far_hi, w1 = after((far_hi, w1))
    t0, t1, t2 = call(product_kernel, (a_hi, near_hi, far_hi, *core_swaps(far_hi, 2), w1), halves)
    up = shifted(t0, hop1)
    far_lo, t1 = after((far_lo, t1))
    u0, u1, u2 = call(product_kernel, (a_lo, near_lo, far_lo, *core_swaps(far_lo, 2), w1), halves)
    down = shifted(u2, -hop1)
    s_lo, a_lo = call(join_kernel, (s_lo, u1, up, t2, vec1), halves[:2])
    from_low = shifted(a_lo, hop2)
    from_high = shifted(a_lo, -hop2)
    ch, a_lo = after((ch, a_lo))
    w2 = staged(2, ch, conv_weight)
    s_hi, a_hi = call(join_kernel, (s_hi, t1, u0, down, vec1), halves[:2])
    far_hi = chip_swap(a_hi)
    near_hi = core_swap(a_hi)
    far_hi, from_low, from_high, w2 = after((far_hi, from_low, from_high, w2))
    a_lo, a_hi = after((a_lo, a_hi))

    far_own = chip_swap(a_lo)
    near_own = core_swap(a_lo)
    near_low = core_swap(from_low)
    near_high = core_swap(from_high)
    g_hi = [a_hi, near_hi, far_hi, *core_swaps(far_hi, 2)]
    *g_hi, far_own, near_own, near_low, near_high = after((*g_hi, far_own, near_own, near_low, near_high))
    q0, q_hi, q2 = call(product_kernel, (*g_hi, w2), halves)
    up_hi = shifted(q0, hop2)
    down_hi = shifted(q2, -hop2)
    from_low, from_high, far_own, q_hi = after((from_low, from_high, far_own, q_hi))
    far_low = chip_swap(from_low)
    far_high = chip_swap(from_high)
    g_own = (a_lo, near_own, far_own, core_swap(far_own))
    g_low = (from_low, near_low, far_low, core_swap(far_low))
    g_high = (from_high, near_high, far_high, core_swap(far_high))
    (part,) = call(part_kernel, (*g_own, *g_low, s_lo, vec2, w2), halves[:1], dtype=F32)
    (upper,) = call(upper_kernel, (s_hi, q_hi, up_hi, down_hi, vec2), halves[:1], flops=COST)
    (out,) = call(out_kernel, (*g_high, part, upper, w2), [ROWS])
    return out


def solution(mesh):
    return jax.shard_map(
        per_device,
        mesh=mesh,
        in_specs=(
            P("seq", "ch"),
            P(None, "ch"),
            P(None, "ch"),
            P(None, None, None, "ch"),
            P(None, "ch"),
        ),
        out_specs=P("seq", "ch"),
        check_vma=False,
    )
```

```python
import functools

import jax
import jax.numpy as jnp
from jax import lax
from jax.experimental import pallas as pl
from jax.experimental.pallas import tpu as pltpu
from jax.sharding import PartitionSpec as P

F32 = jnp.float32
BF16 = jnp.bfloat16
ERFC = (
    -1.26551223, 1.00002368, 0.37409196, 0.09678418, -0.18628806,
    0.27886807, -1.13520398, 1.48851587, -0.82215223, 0.17087277,
)
ROWS = 1024
MID = ROWS // 2
W = 384
R = 64
FIRST = MID - R
COST = 10**10
JOIN_COST = 3 * 10**9
VMEM = pl.BlockSpec(memory_space=pltpu.VMEM)
SMEM = pl.BlockSpec(memory_space=pltpu.SMEM)
HBM = pl.BlockSpec(memory_space=pltpu.HBM)


def gelu(x):
    z = jnp.abs(x) * 0.7071067811865476
    t = 1.0 / (1.0 + 0.5 * z)
    poly = jnp.full_like(t, ERFC[-1])
    for c in ERFC[-2::-1]:
        poly = poly * t + c
    e = t * jnp.exp(poly - z * z)
    return 0.5 * x * jnp.where(x >= 0.0, 2.0 - e, e)


def shifted(array, by):
    size = lax.axis_size("seq")
    pairs = [(i, i + by) for i in range(size) if 0 <= i + by < size]
    return lax.ppermute(array, "seq", pairs)


def chip_swap(array):
    return lax.ppermute(array, "ch", [(i, i ^ 2) for i in range(4)])


def core_swap(array):
    return lax.ppermute(array, "ch", [(i, i ^ 1) for i in range(4)])


def core_swaps(array, parts):
    n = array.shape[0] // parts
    return [core_swap(array[i * n : i * n + n]) for i in range(parts)]


def dot(a, b):
    return jnp.dot(a, b, preferred_element_type=F32)


def stage_kernel(layer, ch_ref, w_hbm, o_ref, sems):
    copies = []
    for k in range(3):
        for p in range(4):
            row = pl.multiple_of((ch_ref[0] ^ p) * W, 128)
            copies.append(
                pltpu.make_async_copy(
                    w_hbm.at[layer, k, pl.ds(row, W), :],
                    o_ref.at[pl.ds(p * W, W), pl.ds(k * W, W)],
                    sems.at[len(copies)],
                )
            )
    for copy in copies:
        copy.start()
    for copy in copies:
        copy.wait()


def finish(total, vec_ref, s_ref, a_ref):
    s = (total + vec_ref[0:1, :]).astype(BF16)
    s_ref[...] = s
    a_ref[...] = gelu(s.astype(F32) * vec_ref[1:2, :] + vec_ref[2:3, :]).astype(BF16)


def near_kernel(plan, parts, first_row, *refs):
    groups, at = [], 0
    for part in parts:
        group = refs[at : at + 3 + part]
        groups.append([[group[0]], [group[1]], [group[2]], group[3:]])
        at += 3 + part
    bins_ref, vec_ref, w_ref, s_ref, a_ref, buf = refs[at:]
    to = 0
    for g, at, count in plan:
        for p, pieces in enumerate(groups[g]):
            low = 0
            for piece in pieces:
                start, stop = max(at, low), min(at + count, low + piece.shape[0])
                if start < stop:
                    buf[to + start - at : to + stop - at, p * W : (p + 1) * W] = piece[start - low : stop - low, :]
                low += piece.shape[0]
        to += count
    total = bins_ref[first_row : first_row + MID, :].astype(F32)
    for k in range(3):
        total = total + dot(buf[k * R : k * R + MID, :], w_ref[:, k * W : (k + 1) * W])
    finish(total, vec_ref, s_ref, a_ref)


def product_kernel(*refs):
    pieces, (w_ref, o0, o1, o2) = refs[:-4], refs[-4:]
    full = dot(joined(pieces), w_ref[...])
    for k, o in enumerate((o0, o1, o2)):
        o[...] = full[:, k * W : (k + 1) * W].astype(BF16)


def join_kernel(s0, t0, t1, t2, vec_ref, s_ref, a_ref):
    f = lambda ref: ref[...].astype(F32)
    finish(f(s0) + f(t0) + f(t1) + f(t2), vec_ref, s_ref, a_ref)


def early_join_kernel(s0, up, t2, o_ref):
    o_ref[...] = s0[...].astype(F32) + up[...].astype(F32) + t2[...].astype(F32)


def late_join_kernel(part, t1, vec_ref, s_ref, a_ref):
    finish(part[...] + t1[...].astype(F32), vec_ref, s_ref, a_ref)


def joined(refs, fars=1):
    far = jnp.concatenate([p[...] for p in refs[2 : 2 + fars]], axis=0)
    near_far = jnp.concatenate([p[...] for p in refs[2 + fars :]], axis=0)
    return jnp.concatenate([refs[0][...], refs[1][...], far, near_far], axis=1)


def rims_kernel(low_ref, high_ref, o_ref):
    o_ref[:R, :] = low_ref[...]
    o_ref[R:, :] = high_ref[...]


def part_kernel(*refs):
    own, low, (s_ref, vec_ref, w_ref, o_ref) = refs[:4], refs[4:8], refs[8:]
    total = s_ref[...].astype(F32) + vec_ref[0:1, :]
    total = total + dot(joined(own, 1), w_ref[:, W : 2 * W])
    o_ref[...] = total + dot(joined(low, 1), w_ref[:, 0:W])


def upper_kernel(s_hi, q_hi, up_hi, down_hi, vec_ref, o_ref):
    total = vec_ref[0:1, :]
    for ref in (s_hi, q_hi, up_hi, down_hi):
        total = total + ref[...].astype(F32)
    o_ref[...] = total.astype(BF16)


def out_kernel(*refs):
    high, (part, upper, w_ref, o_ref) = refs[:4], refs[4:]
    o_ref[:MID, :] = (part[...] + dot(joined(high), w_ref[:, 2 * W : 3 * W])).astype(BF16)
    o_ref[MID:, :] = upper[...]


def call(kernel, args, rows, scratch=(), dtype=BF16, flops=0):
    return pl.pallas_call(
        kernel,
        out_shape=[jax.ShapeDtypeStruct((r, W), dtype) for r in rows],
        in_specs=[VMEM] * len(args),
        out_specs=[VMEM] * len(rows),
        scratch_shapes=list(scratch),
        compiler_params=pltpu.CompilerParams(vmem_limit_bytes=20 * 1024 * 1024),
        cost_estimate=pl.CostEstimate(flops=flops, bytes_accessed=1024, transcendentals=0),
    )(*args)


def staged(layer, ch, conv_weight):
    return pl.pallas_call(
        functools.partial(stage_kernel, layer),
        out_shape=jax.ShapeDtypeStruct((4 * W, 3 * W), BF16),
        in_specs=[SMEM, HBM],
        out_specs=VMEM,
        scratch_shapes=[pltpu.SemaphoreType.DMA((12,))],
        compiler_params=pltpu.CompilerParams(vmem_limit_bytes=50 * 1024 * 1024),
    )(ch, conv_weight)


def per_device(bins_in, pre_scale, pre_shift, conv_weight, conv_bias):
    after = lax.optimization_barrier
    ch = lax.axis_index("ch").astype(jnp.int32).reshape(1)
    hop1, hop2 = 1, 4096 // ROWS
    vec0 = jnp.stack([conv_bias[0], pre_scale[1], pre_shift[1]])
    vec1 = jnp.stack([conv_bias[1], pre_scale[2], pre_shift[2]])
    vec2 = conv_bias[2:3]
    halves = [MID] * 3
    scratch = [pltpu.VMEM((MID + 2 * R, 4 * W), BF16)]

    def entry(x):
        return gelu(x.astype(F32) * pre_scale[0] + pre_shift[0]).astype(BF16)

    act_1 = entry(bins_in[FIRST:])
    far_1 = chip_swap(act_1)
    near_1 = core_swap(act_1)
    act_3 = entry(bins_in[:FIRST])
    low = shifted(act_1[-R:], 1)
    high = shifted(act_3[:R], -1)
    w0 = staged(0, ch, conv_weight)
    low, high, w0 = after((low, high, w0))
    (act_2,) = call(rims_kernel, (low, high), [2 * R])
    act_2, act_3 = after((act_2, act_3))
    far_2 = chip_swap(act_2)
    near_2 = core_swap(act_2)
    far_3 = chip_swap(act_3)
    near_3 = core_swap(act_3)
    far_1, far_2, near_1 = after((far_1, far_2, near_1))
    g_1 = (act_1, near_1, far_1, *core_swaps(far_1, 2))
    g_2 = (act_2, near_2, far_2, core_swap(far_2))
    g_1, g_2, far_3 = after((g_1, g_2, far_3))
    plan_hi = ((0, 0, ROWS - FIRST), (1, R, R))
    s_hi, a_hi = call(
        functools.partial(near_kernel, plan_hi, (2, 1), MID), (*g_1, *g_2, bins_in, vec0, w0), halves[:2], scratch
    )
    far_hi = chip_swap(a_hi)
    near_hi = core_swap(a_hi)
    near_3, a_hi = after((near_3, a_hi))
    g_3 = (act_3, near_3, far_3, core_swap(far_3))
    plan_lo = ((1, 0, R), (2, 0, FIRST), (0, 0, 2 * R))
    s_lo, a_lo = call(
        functools.partial(near_kernel, plan_lo, (2, 1, 1), 0), (*g_1, *g_2, *g_3, bins_in, vec0, w0), halves[:2], scratch
    )
    far_lo = chip_swap(a_lo)
    near_lo = core_swap(a_lo)

    ch, a_lo = after((ch, a_lo))
    w1 = staged(1, ch, conv_weight)
    far_hi, w1 = after((far_hi, w1))
    t0, t1, t2 = call(product_kernel, (a_hi, near_hi, far_hi, *core_swaps(far_hi, 2), w1), halves)
    up = shifted(t0, hop1)
    far_lo, t1 = after((far_lo, t1))
    u0, u1, u2 = call(product_kernel, (a_lo, near_lo, far_lo, *core_swaps(far_lo, 2), w1), halves)
    down = shifted(u2, -hop1)
    (early,) = call(early_join_kernel, (s_lo, up, t2), halves[:1], dtype=F32, flops=JOIN_COST)
    s_lo, a_lo = call(late_join_kernel, (early, u1, vec1), halves[:2])
    from_low = shifted(a_lo, hop2)
    from_high = shifted(a_lo, -hop2)
    ch, a_lo = after((ch, a_lo))
    w2 = staged(2, ch, conv_weight)
    s_hi, a_hi = call(join_kernel, (s_hi, t1, u0, down, vec1), halves[:2])
    far_hi = chip_swap(a_hi)
    near_hi = core_swap(a_hi)
    near_own = core_swap(a_lo)
    far_hi, from_low, from_high, near_own, a_lo, w2 = after((far_hi, from_low, from_high, near_own, a_lo, w2))

    far_own = chip_swap(a_lo)
    near_low = core_swap(from_low)
    near_high = core_swap(from_high)
    g_hi = [a_hi, near_hi, far_hi, *core_swaps(far_hi, 2)]
    *g_hi, near_low, near_high = after((*g_hi, near_low, near_high))
    q0, q_hi, q2 = call(product_kernel, (*g_hi, w2), halves)
    up_hi = shifted(q0, hop2)
    down_hi = shifted(q2, -hop2)
    from_low, from_high, q_hi = after((from_low, from_high, q_hi))
    far_low = chip_swap(from_low)
    far_high = chip_swap(from_high)
    g_own = (a_lo, near_own, far_own, core_swap(far_own))
    g_low = (from_low, near_low, far_low, core_swap(far_low))
    g_high = (from_high, near_high, far_high, core_swap(far_high))
    (part,) = call(part_kernel, (*g_own, *g_low, s_lo, vec2, w2), halves[:1], dtype=F32)
    (upper,) = call(upper_kernel, (s_hi, q_hi, up_hi, down_hi, vec2), halves[:1], flops=COST)
    (out,) = call(out_kernel, (*g_high, part, upper, w2), [ROWS])
    return out


def solution(mesh):
    return jax.shard_map(
        per_device,
        mesh=mesh,
        in_specs=(
            P("seq", "ch"),
            P(None, "ch"),
            P(None, "ch"),
            P(None, None, None, "ch"),
            P(None, "ch"),
        ),
        out_specs=P("seq", "ch"),
        check_vma=False,
    )
```

```python
import functools

import jax
import jax.numpy as jnp
from jax import lax
from jax.experimental import pallas as pl
from jax.experimental.pallas import tpu as pltpu
from jax.sharding import PartitionSpec as P

F32 = jnp.float32
BF16 = jnp.bfloat16
ERFC = (
    -1.26551223, 1.00002368, 0.37409196, 0.09678418, -0.18628806,
    0.27886807, -1.13520398, 1.48851587, -0.82215223, 0.17087277,
)
ROWS = 1024
MID = ROWS // 2
W = 384
R = 64
FIRST = MID - R
COST = 10**10
RIM_COST = 10**10
JOIN_COST = 3 * 10**9
VMEM = pl.BlockSpec(memory_space=pltpu.VMEM)
SMEM = pl.BlockSpec(memory_space=pltpu.SMEM)
HBM = pl.BlockSpec(memory_space=pltpu.HBM)


def gelu(x):
    z = jnp.abs(x) * 0.7071067811865476
    t = 1.0 / (1.0 + 0.5 * z)
    poly = jnp.full_like(t, ERFC[-1])
    for c in ERFC[-2::-1]:
        poly = poly * t + c
    e = t * jnp.exp(poly - z * z)
    return 0.5 * x * jnp.where(x >= 0.0, 2.0 - e, e)


def shifted(array, by):
    size = lax.axis_size("seq")
    pairs = [(i, i + by) for i in range(size) if 0 <= i + by < size]
    return lax.ppermute(array, "seq", pairs)


def chip_swap(array):
    return lax.ppermute(array, "ch", [(i, i ^ 2) for i in range(4)])


def core_swap(array):
    return lax.ppermute(array, "ch", [(i, i ^ 1) for i in range(4)])


def core_swaps(array, parts):
    n = array.shape[0] // parts
    return [core_swap(array[i * n : i * n + n]) for i in range(parts)]


def dot(a, b):
    return jnp.dot(a, b, preferred_element_type=F32)


def stage_kernel(layer, ch_ref, w_hbm, o_ref, sems):
    copies = []
    for k in range(3):
        for p in range(4):
            row = pl.multiple_of((ch_ref[0] ^ p) * W, 128)
            copies.append(
                pltpu.make_async_copy(
                    w_hbm.at[layer, k, pl.ds(row, W), :],
                    o_ref.at[pl.ds(p * W, W), pl.ds(k * W, W)],
                    sems.at[len(copies)],
                )
            )
    for copy in copies:
        copy.start()
    for copy in copies:
        copy.wait()


def finish(total, vec_ref, s_ref, a_ref):
    s = (total + vec_ref[0:1, :]).astype(BF16)
    s_ref[...] = s
    a_ref[...] = gelu(s.astype(F32) * vec_ref[1:2, :] + vec_ref[2:3, :]).astype(BF16)


def near_kernel(plan, parts, first_row, *refs):
    groups, at = [], 0
    for part in parts:
        group = refs[at : at + 3 + part]
        groups.append([[group[0]], [group[1]], [group[2]], group[3:]])
        at += 3 + part
    bins_ref, vec_ref, w_ref, s_ref, a_ref, buf = refs[at:]
    to = 0
    for g, at, count in plan:
        for p, pieces in enumerate(groups[g]):
            low = 0
            for piece in pieces:
                start, stop = max(at, low), min(at + count, low + piece.shape[0])
                if start < stop:
                    buf[to + start - at : to + stop - at, p * W : (p + 1) * W] = piece[start - low : stop - low, :]
                low += piece.shape[0]
        to += count
    total = bins_ref[first_row : first_row + MID, :].astype(F32)
    for k in range(3):
        total = total + dot(buf[k * R : k * R + MID, :], w_ref[:, k * W : (k + 1) * W])
    finish(total, vec_ref, s_ref, a_ref)


def product_kernel(*refs):
    pieces, (w_ref, o0, o1, o2) = refs[:-4], refs[-4:]
    full = dot(joined(pieces), w_ref[...])
    for k, o in enumerate((o0, o1, o2)):
        o[...] = full[:, k * W : (k + 1) * W].astype(BF16)


def join_kernel(s0, t0, t1, t2, vec_ref, s_ref, a_ref):
    f = lambda ref: ref[...].astype(F32)
    finish(f(s0) + f(t0) + f(t1) + f(t2), vec_ref, s_ref, a_ref)


def early_join_kernel(s0, up, t2, o_ref):
    o_ref[...] = s0[...].astype(F32) + up[...].astype(F32) + t2[...].astype(F32)


def late_join_kernel(part, t1, vec_ref, s_ref, a_ref):
    finish(part[...] + t1[...].astype(F32), vec_ref, s_ref, a_ref)


def joined(refs, fars=1):
    far = jnp.concatenate([p[...] for p in refs[2 : 2 + fars]], axis=0)
    near_far = jnp.concatenate([p[...] for p in refs[2 + fars :]], axis=0)
    return jnp.concatenate([refs[0][...], refs[1][...], far, near_far], axis=1)


def rims_kernel(low_ref, high_ref, o_ref):
    o_ref[:R, :] = low_ref[...]
    o_ref[R:, :] = high_ref[...]


def part_kernel(*refs):
    own, low, (s_ref, vec_ref, w_ref, o_ref) = refs[:4], refs[4:8], refs[8:]
    total = s_ref[...].astype(F32) + vec_ref[0:1, :]
    total = total + dot(joined(own, 1), w_ref[:, W : 2 * W])
    o_ref[...] = total + dot(joined(low, 1), w_ref[:, 0:W])


def upper_kernel(s_hi, q_hi, up_hi, down_hi, vec_ref, o_ref):
    total = vec_ref[0:1, :]
    for ref in (s_hi, q_hi, up_hi, down_hi):
        total = total + ref[...].astype(F32)
    o_ref[...] = total.astype(BF16)


def out_kernel(*refs):
    high, (part, upper, w_ref, o_ref) = refs[:4], refs[4:]
    o_ref[:MID, :] = (part[...] + dot(joined(high), w_ref[:, 2 * W : 3 * W])).astype(BF16)
    o_ref[MID:, :] = upper[...]


def call(kernel, args, rows, scratch=(), dtype=BF16, flops=0):
    return pl.pallas_call(
        kernel,
        out_shape=[jax.ShapeDtypeStruct((r, W), dtype) for r in rows],
        in_specs=[VMEM] * len(args),
        out_specs=[VMEM] * len(rows),
        scratch_shapes=list(scratch),
        compiler_params=pltpu.CompilerParams(vmem_limit_bytes=20 * 1024 * 1024),
        cost_estimate=pl.CostEstimate(flops=flops, bytes_accessed=1024, transcendentals=0),
    )(*args)


def staged(layer, ch, conv_weight):
    return pl.pallas_call(
        functools.partial(stage_kernel, layer),
        out_shape=jax.ShapeDtypeStruct((4 * W, 3 * W), BF16),
        in_specs=[SMEM, HBM],
        out_specs=VMEM,
        scratch_shapes=[pltpu.SemaphoreType.DMA((12,))],
        compiler_params=pltpu.CompilerParams(vmem_limit_bytes=50 * 1024 * 1024),
    )(ch, conv_weight)


def per_device(bins_in, pre_scale, pre_shift, conv_weight, conv_bias):
    after = lax.optimization_barrier
    ch = lax.axis_index("ch").astype(jnp.int32).reshape(1)
    hop1, hop2 = 1, 4096 // ROWS
    vec0 = jnp.stack([conv_bias[0], pre_scale[1], pre_shift[1]])
    vec1 = jnp.stack([conv_bias[1], pre_scale[2], pre_shift[2]])
    vec2 = conv_bias[2:3]
    halves = [MID] * 3
    scratch = [pltpu.VMEM((MID + 2 * R, 4 * W), BF16)]

    def entry(x):
        return gelu(x.astype(F32) * pre_scale[0] + pre_shift[0]).astype(BF16)

    rim = entry(jnp.concatenate([bins_in[ROWS - R :], bins_in[:R]], axis=0))
    low = shifted(rim[:R], 1)
    high = shifted(rim[R:], -1)
    (act_2,) = call(rims_kernel, (low, high), [2 * R], flops=RIM_COST)
    act_1 = entry(bins_in[FIRST:])
    far_1 = chip_swap(act_1)
    near_1 = core_swap(act_1)
    act_3 = entry(bins_in[:FIRST])
    w0 = staged(0, ch, conv_weight)
    act_2, act_3 = after((act_2, act_3))
    far_2 = chip_swap(act_2)
    near_2 = core_swap(act_2)
    far_3 = chip_swap(act_3)
    near_3 = core_swap(act_3)
    far_1, far_2, near_1 = after((far_1, far_2, near_1))
    g_1 = (act_1, near_1, far_1, *core_swaps(far_1, 2))
    g_2 = (act_2, near_2, far_2, core_swap(far_2))
    g_1, g_2, far_3 = after((g_1, g_2, far_3))
    plan_hi = ((0, 0, ROWS - FIRST), (1, R, R))
    s_hi, a_hi = call(
        functools.partial(near_kernel, plan_hi, (2, 1), MID), (*g_1, *g_2, bins_in, vec0, w0), halves[:2], scratch
    )
    far_hi = chip_swap(a_hi)
    near_hi = core_swap(a_hi)
    near_3, a_hi = after((near_3, a_hi))
    g_3 = (act_3, near_3, far_3, core_swap(far_3))
    plan_lo = ((1, 0, R), (2, 0, FIRST), (0, 0, 2 * R))
    s_lo, a_lo = call(
        functools.partial(near_kernel, plan_lo, (2, 1, 1), 0), (*g_1, *g_2, *g_3, bins_in, vec0, w0), halves[:2], scratch
    )
    far_lo = chip_swap(a_lo)
    near_lo = core_swap(a_lo)

    ch, a_lo = after((ch, a_lo))
    w1 = staged(1, ch, conv_weight)
    far_hi, w1 = after((far_hi, w1))
    t0, t1, t2 = call(product_kernel, (a_hi, near_hi, far_hi, *core_swaps(far_hi, 2), w1), halves)
    up = shifted(t0, hop1)
    far_lo, t1 = after((far_lo, t1))
    u0, u1, u2 = call(product_kernel, (a_lo, near_lo, far_lo, *core_swaps(far_lo, 2), w1), halves)
    down = shifted(u2, -hop1)
    (early,) = call(early_join_kernel, (s_lo, up, t2), halves[:1], dtype=F32, flops=JOIN_COST)
    s_lo, a_lo = call(late_join_kernel, (early, u1, vec1), halves[:2])
    from_low = shifted(a_lo, hop2)
    from_high = shifted(a_lo, -hop2)
    ch, a_lo = after((ch, a_lo))
    w2 = staged(2, ch, conv_weight)
    s_hi, a_hi = call(join_kernel, (s_hi, t1, u0, down, vec1), halves[:2])
    far_hi = chip_swap(a_hi)
    near_hi = core_swap(a_hi)
    near_own = core_swap(a_lo)
    far_hi, from_low, from_high, near_own, a_lo, w2 = after((far_hi, from_low, from_high, near_own, a_lo, w2))

    far_own = chip_swap(a_lo)
    near_low = core_swap(from_low)
    near_high = core_swap(from_high)
    g_hi = [a_hi, near_hi, far_hi, *core_swaps(far_hi, 2)]
    *g_hi, near_low, near_high = after((*g_hi, near_low, near_high))
    q0, q_hi, q2 = call(product_kernel, (*g_hi, w2), halves)
    up_hi = shifted(q0, hop2)
    down_hi = shifted(q2, -hop2)
    from_low, from_high, q_hi = after((from_low, from_high, q_hi))
    far_low = chip_swap(from_low)
    far_high = chip_swap(from_high)
    g_own = (a_lo, near_own, far_own, core_swap(far_own))
    g_low = (from_low, near_low, far_low, core_swap(far_low))
    g_high = (from_high, near_high, far_high, core_swap(far_high))
    (part,) = call(part_kernel, (*g_own, *g_low, s_lo, vec2, w2), halves[:1], dtype=F32)
    (upper,) = call(upper_kernel, (s_hi, q_hi, up_hi, down_hi, vec2), halves[:1], flops=COST)
    (out,) = call(out_kernel, (*g_high, part, upper, w2), [ROWS])
    return out


def solution(mesh):
    return jax.shard_map(
        per_device,
        mesh=mesh,
        in_specs=(
            P("seq", "ch"),
            P(None, "ch"),
            P(None, "ch"),
            P(None, None, None, "ch"),
            P(None, "ch"),
        ),
        out_specs=P("seq", "ch"),
        check_vma=False,
    )
```

```python
import functools

import jax
import jax.numpy as jnp
from jax import lax
from jax.experimental import pallas as pl
from jax.experimental.pallas import tpu as pltpu
from jax.sharding import PartitionSpec as P

F32 = jnp.float32
BF16 = jnp.bfloat16
ERFC = (
    -1.26551223, 1.00002368, 0.37409196, 0.09678418, -0.18628806,
    0.27886807, -1.13520398, 1.48851587, -0.82215223, 0.17087277,
)
ROWS = 1024
MID = ROWS // 2
W = 384
R = 64
FIRST = MID - R
COST = 10**10
RIM_COST = 10**10
JOIN_COST = 3 * 10**9
VMEM = pl.BlockSpec(memory_space=pltpu.VMEM)
SMEM = pl.BlockSpec(memory_space=pltpu.SMEM)
HBM = pl.BlockSpec(memory_space=pltpu.HBM)


def gelu(x):
    z = jnp.abs(x) * 0.7071067811865476
    t = 1.0 / (1.0 + 0.5 * z)
    poly = jnp.full_like(t, ERFC[-1])
    for c in ERFC[-2::-1]:
        poly = poly * t + c
    e = t * jnp.exp(poly - z * z)
    return 0.5 * x * jnp.where(x >= 0.0, 2.0 - e, e)


def shifted(array, by):
    size = lax.axis_size("seq")
    pairs = [(i, i + by) for i in range(size) if 0 <= i + by < size]
    return lax.ppermute(array, "seq", pairs)


def chip_swap(array):
    return lax.ppermute(array, "ch", [(i, i ^ 2) for i in range(4)])


def core_swap(array):
    return lax.ppermute(array, "ch", [(i, i ^ 1) for i in range(4)])


def core_swaps(array, parts):
    n = array.shape[0] // parts
    return [core_swap(array[i * n : i * n + n]) for i in range(parts)]


def dot(a, b):
    return jnp.dot(a, b, preferred_element_type=F32)


def stage_kernel(layer, ch_ref, w_hbm, o_ref, sems):
    copies = []
    for k in range(3):
        for p in range(4):
            row = pl.multiple_of((ch_ref[0] ^ p) * W, 128)
            copies.append(
                pltpu.make_async_copy(
                    w_hbm.at[layer, k, pl.ds(row, W), :],
                    o_ref.at[pl.ds(p * W, W), pl.ds(k * W, W)],
                    sems.at[len(copies)],
                )
            )
    for copy in copies:
        copy.start()
    for copy in copies:
        copy.wait()


def finish(total, vec_ref, s_ref, a_ref):
    s = (total + vec_ref[0:1, :]).astype(BF16)
    s_ref[...] = s
    a_ref[...] = gelu(s.astype(F32) * vec_ref[1:2, :] + vec_ref[2:3, :]).astype(BF16)


def near_kernel(plan, parts, first_row, *refs):
    groups, at = [], 0
    for part in parts:
        group = refs[at : at + 3 + part]
        groups.append([[group[0]], [group[1]], [group[2]], group[3:]])
        at += 3 + part
    bins_ref, vec_ref, w_ref, s_ref, a_ref, buf = refs[at:]
    to = 0
    for g, at, count in plan:
        for p, pieces in enumerate(groups[g]):
            low = 0
            for piece in pieces:
                start, stop = max(at, low), min(at + count, low + piece.shape[0])
                if start < stop:
                    buf[to + start - at : to + stop - at, p * W : (p + 1) * W] = piece[start - low : stop - low, :]
                low += piece.shape[0]
        to += count
    total = bins_ref[first_row : first_row + MID, :].astype(F32)
    for k in range(3):
        total = total + dot(buf[k * R : k * R + MID, :], w_ref[:, k * W : (k + 1) * W])
    finish(total, vec_ref, s_ref, a_ref)


def product_kernel(*refs):
    pieces, (w_ref, o0, o1, o2) = refs[:-4], refs[-4:]
    full = dot(joined(pieces), w_ref[...])
    for k, o in enumerate((o0, o1, o2)):
        o[...] = full[:, k * W : (k + 1) * W].astype(BF16)


def join_kernel(s0, t0, t1, t2, vec_ref, s_ref, a_ref):
    f = lambda ref: ref[...].astype(F32)
    finish(f(s0) + f(t0) + f(t1) + f(t2), vec_ref, s_ref, a_ref)


def early_join_kernel(s0, up, t2, o_ref):
    o_ref[...] = s0[...].astype(F32) + up[...].astype(F32) + t2[...].astype(F32)


def late_join_kernel(part, t1, vec_ref, s_ref, a_ref):
    finish(part[...] + t1[...].astype(F32), vec_ref, s_ref, a_ref)


def joined(refs, fars=1):
    far = jnp.concatenate([p[...] for p in refs[2 : 2 + fars]], axis=0)
    near_far = jnp.concatenate([p[...] for p in refs[2 + fars :]], axis=0)
    return jnp.concatenate([refs[0][...], refs[1][...], far, near_far], axis=1)


def rims_kernel(low_ref, high_ref, o_ref):
    o_ref[:R, :] = low_ref[...]
    o_ref[R:, :] = high_ref[...]


def part_kernel(*refs):
    own, low, (s_ref, vec_ref, w_ref, o_ref) = refs[:4], refs[4:8], refs[8:]
    total = s_ref[...].astype(F32) + vec_ref[0:1, :]
    total = total + dot(joined(own, 1), w_ref[:, W : 2 * W])
    o_ref[...] = total + dot(joined(low, 1), w_ref[:, 0:W])


def upper_kernel(s_hi, q_hi, up_hi, down_hi, vec_ref, o_ref):
    total = vec_ref[0:1, :]
    for ref in (s_hi, q_hi, up_hi, down_hi):
        total = total + ref[...].astype(F32)
    o_ref[...] = total.astype(BF16)


def out_kernel(*refs):
    high, (part, upper, w_ref, o_ref) = refs[:4], refs[4:]
    o_ref[:MID, :] = (part[...] + dot(joined(high), w_ref[:, 2 * W : 3 * W])).astype(BF16)
    o_ref[MID:, :] = upper[...]


def call(kernel, args, rows, scratch=(), dtype=BF16, flops=0):
    return pl.pallas_call(
        kernel,
        out_shape=[jax.ShapeDtypeStruct((r, W), dtype) for r in rows],
        in_specs=[VMEM] * len(args),
        out_specs=[VMEM] * len(rows),
        scratch_shapes=list(scratch),
        compiler_params=pltpu.CompilerParams(vmem_limit_bytes=20 * 1024 * 1024),
        cost_estimate=pl.CostEstimate(flops=flops, bytes_accessed=1024, transcendentals=0),
    )(*args)


def staged(layer, ch, conv_weight):
    return pl.pallas_call(
        functools.partial(stage_kernel, layer),
        out_shape=jax.ShapeDtypeStruct((4 * W, 3 * W), BF16),
        in_specs=[SMEM, HBM],
        out_specs=VMEM,
        scratch_shapes=[pltpu.SemaphoreType.DMA((12,))],
        compiler_params=pltpu.CompilerParams(vmem_limit_bytes=50 * 1024 * 1024),
    )(ch, conv_weight)


def per_device(bins_in, pre_scale, pre_shift, conv_weight, conv_bias):
    after = lax.optimization_barrier
    ch = lax.axis_index("ch").astype(jnp.int32).reshape(1)
    hop1, hop2 = 1, 4096 // ROWS
    vec0 = jnp.stack([conv_bias[0], pre_scale[1], pre_shift[1]])
    vec1 = jnp.stack([conv_bias[1], pre_scale[2], pre_shift[2]])
    vec2 = conv_bias[2:3]
    halves = [MID] * 3
    scratch = [pltpu.VMEM((MID + 2 * R, 4 * W), BF16)]

    def entry(x):
        return gelu(x.astype(F32) * pre_scale[0] + pre_shift[0]).astype(BF16)

    rim = entry(jnp.concatenate([bins_in[ROWS - R :], bins_in[:R]], axis=0))
    low = shifted(rim[:R], 1)
    high = shifted(rim[R:], -1)
    act_1 = entry(bins_in[FIRST:])
    far_1 = chip_swap(act_1)
    near_1 = core_swap(act_1)
    act_3 = entry(bins_in[:FIRST])
    w0 = staged(0, ch, conv_weight)
    low, high, w0 = after((low, high, w0))
    (act_2,) = call(rims_kernel, (low, high), [2 * R], flops=RIM_COST)
    act_2, act_3 = after((act_2, act_3))
    far_2 = chip_swap(act_2)
    near_2 = core_swap(act_2)
    far_3 = chip_swap(act_3)
    near_3 = core_swap(act_3)
    far_1, far_2, near_1 = after((far_1, far_2, near_1))
    g_1 = (act_1, near_1, far_1, *core_swaps(far_1, 2))
    g_2 = (act_2, near_2, far_2, core_swap(far_2))
    plan_hi = ((0, 0, ROWS - FIRST), (1, R, R))
    s_hi, a_hi = call(
        functools.partial(near_kernel, plan_hi, (2, 1), MID), (*g_1, *g_2, bins_in, vec0, w0), halves[:2], scratch
    )
    far_hi = chip_swap(a_hi)
    near_hi = core_swap(a_hi)
    near_3, a_hi = after((near_3, a_hi))
    g_3 = (act_3, near_3, far_3, core_swap(far_3))
    plan_lo = ((1, 0, R), (2, 0, FIRST), (0, 0, 2 * R))
    s_lo, a_lo = call(
        functools.partial(near_kernel, plan_lo, (2, 1, 1), 0), (*g_1, *g_2, *g_3, bins_in, vec0, w0), halves[:2], scratch
    )
    far_lo = chip_swap(a_lo)
    near_lo = core_swap(a_lo)

    ch, a_lo = after((ch, a_lo))
    w1 = staged(1, ch, conv_weight)
    far_hi, w1 = after((far_hi, w1))
    t0, t1, t2 = call(product_kernel, (a_hi, near_hi, far_hi, *core_swaps(far_hi, 2), w1), halves)
    up = shifted(t0, hop1)
    far_lo, t1 = after((far_lo, t1))
    u0, u1, u2 = call(product_kernel, (a_lo, near_lo, far_lo, *core_swaps(far_lo, 2), w1), halves)
    down = shifted(u2, -hop1)
    (early,) = call(early_join_kernel, (s_lo, up, t2), halves[:1], dtype=F32, flops=JOIN_COST)
    s_lo, a_lo = call(late_join_kernel, (early, u1, vec1), halves[:2])
    from_low = shifted(a_lo, hop2)
    from_high = shifted(a_lo, -hop2)
    ch, a_lo = after((ch, a_lo))
    w2 = staged(2, ch, conv_weight)
    s_hi, a_hi = call(join_kernel, (s_hi, t1, u0, down, vec1), halves[:2])
    far_hi = chip_swap(a_hi)
    near_hi = core_swap(a_hi)
    near_own = core_swap(a_lo)
    far_hi, from_low, from_high, near_own, a_lo, w2 = after((far_hi, from_low, from_high, near_own, a_lo, w2))

    far_own = chip_swap(a_lo)
    near_low = core_swap(from_low)
    near_high = core_swap(from_high)
    g_hi = [a_hi, near_hi, far_hi, *core_swaps(far_hi, 2)]
    *g_hi, near_low, near_high = after((*g_hi, near_low, near_high))
    q0, q_hi, q2 = call(product_kernel, (*g_hi, w2), halves)
    up_hi = shifted(q0, hop2)
    down_hi = shifted(q2, -hop2)
    from_low, from_high, q_hi = after((from_low, from_high, q_hi))
    far_low = chip_swap(from_low)
    far_high = chip_swap(from_high)
    g_own = (a_lo, near_own, far_own, core_swap(far_own))
    g_low = (from_low, near_low, far_low, core_swap(far_low))
    g_high = (from_high, near_high, far_high, core_swap(far_high))
    (part,) = call(part_kernel, (*g_own, *g_low, s_lo, vec2, w2), halves[:1], dtype=F32)
    (upper,) = call(upper_kernel, (s_hi, q_hi, up_hi, down_hi, vec2), halves[:1], flops=COST)
    (out,) = call(out_kernel, (*g_high, part, upper, w2), [ROWS])
    return out


def solution(mesh):
    return jax.shard_map(
        per_device,
        mesh=mesh,
        in_specs=(
            P("seq", "ch"),
            P(None, "ch"),
            P(None, "ch"),
            P(None, None, None, "ch"),
            P(None, "ch"),
        ),
        out_specs=P("seq", "ch"),
        check_vma=False,
    )
```

```python
import functools

import jax
import jax.numpy as jnp
from jax import lax
from jax.experimental import pallas as pl
from jax.experimental.pallas import tpu as pltpu
from jax.sharding import PartitionSpec as P

F32 = jnp.float32
BF16 = jnp.bfloat16
ERFC = (
    -1.26551223, 1.00002368, 0.37409196, 0.09678418, -0.18628806,
    0.27886807, -1.13520398, 1.48851587, -0.82215223, 0.17087277,
)
ROWS = 1024
MID = ROWS // 2
W = 384
R = 64
FIRST = MID - R
COST = 10**10
RIM_COST = 10**10
JOIN_COST = 3 * 10**9
VMEM = pl.BlockSpec(memory_space=pltpu.VMEM)
SMEM = pl.BlockSpec(memory_space=pltpu.SMEM)
HBM = pl.BlockSpec(memory_space=pltpu.HBM)


def gelu(x):
    z = jnp.abs(x) * 0.7071067811865476
    t = 1.0 / (1.0 + 0.5 * z)
    poly = jnp.full_like(t, ERFC[-1])
    for c in ERFC[-2::-1]:
        poly = poly * t + c
    e = t * jnp.exp(poly - z * z)
    return 0.5 * x * jnp.where(x >= 0.0, 2.0 - e, e)


def shifted(array, by):
    size = lax.axis_size("seq")
    pairs = [(i, i + by) for i in range(size) if 0 <= i + by < size]
    return lax.ppermute(array, "seq", pairs)


def chip_swap(array):
    return lax.ppermute(array, "ch", [(i, i ^ 2) for i in range(4)])


def core_swap(array):
    return lax.ppermute(array, "ch", [(i, i ^ 1) for i in range(4)])


def core_swaps(array, parts):
    n = array.shape[0] // parts
    return [core_swap(array[i * n : i * n + n]) for i in range(parts)]


def dot(a, b):
    return jnp.dot(a, b, preferred_element_type=F32)


def stage_kernel(layer, ch_ref, w_hbm, o_ref, sems):
    copies = []
    for k in range(3):
        for p in range(4):
            row = pl.multiple_of((ch_ref[0] ^ p) * W, 128)
            copies.append(
                pltpu.make_async_copy(
                    w_hbm.at[layer, k, pl.ds(row, W), :],
                    o_ref.at[pl.ds(p * W, W), pl.ds(k * W, W)],
                    sems.at[len(copies)],
                )
            )
    for copy in copies:
        copy.start()
    for copy in copies:
        copy.wait()


def finish(total, vec_ref, s_ref, a_ref):
    s = (total + vec_ref[0:1, :]).astype(BF16)
    s_ref[...] = s
    a_ref[...] = gelu(s.astype(F32) * vec_ref[1:2, :] + vec_ref[2:3, :]).astype(BF16)


def near_kernel(plan, parts, first_row, *refs):
    groups, at = [], 0
    for part in parts:
        group = refs[at : at + 3 + part]
        groups.append([[group[0]], [group[1]], [group[2]], group[3:]])
        at += 3 + part
    bins_ref, vec_ref, w_ref, s_ref, a_ref, buf = refs[at:]
    to = 0
    for g, at, count in plan:
        for p, pieces in enumerate(groups[g]):
            low = 0
            for piece in pieces:
                start, stop = max(at, low), min(at + count, low + piece.shape[0])
                if start < stop:
                    buf[to + start - at : to + stop - at, p * W : (p + 1) * W] = piece[start - low : stop - low, :]
                low += piece.shape[0]
        to += count
    total = bins_ref[first_row : first_row + MID, :].astype(F32)
    for k in range(3):
        total = total + dot(buf[k * R : k * R + MID, :], w_ref[:, k * W : (k + 1) * W])
    finish(total, vec_ref, s_ref, a_ref)


def product_kernel(*refs):
    pieces, (w_ref, o0, o1, o2) = refs[:-4], refs[-4:]
    full = dot(joined(pieces), w_ref[...])
    for k, o in enumerate((o0, o1, o2)):
        o[...] = full[:, k * W : (k + 1) * W].astype(BF16)


def join_kernel(s0, t0, t1, t2, vec_ref, s_ref, a_ref):
    f = lambda ref: ref[...].astype(F32)
    finish(f(s0) + f(t0) + f(t1) + f(t2), vec_ref, s_ref, a_ref)


def early_join_kernel(s0, up, t2, o_ref):
    o_ref[...] = s0[...].astype(F32) + up[...].astype(F32) + t2[...].astype(F32)


def late_join_kernel(part, t1, vec_ref, s_ref, a_ref):
    finish(part[...] + t1[...].astype(F32), vec_ref, s_ref, a_ref)


def joined(refs, fars=1):
    far = jnp.concatenate([p[...] for p in refs[2 : 2 + fars]], axis=0)
    near_far = jnp.concatenate([p[...] for p in refs[2 + fars :]], axis=0)
    return jnp.concatenate([refs[0][...], refs[1][...], far, near_far], axis=1)


def rims_kernel(low_ref, high_ref, o_ref):
    o_ref[:R, :] = low_ref[...]
    o_ref[R:, :] = high_ref[...]


def upper_kernel(s_hi, q_hi, up_hi, down_hi, vec_ref, o_ref):
    total = vec_ref[0:1, :]
    for ref in (s_hi, q_hi, up_hi, down_hi):
        total = total + ref[...].astype(F32)
    o_ref[...] = total.astype(BF16)


def out_kernel(*refs):
    own, low, high, (s_lo, upper, vec_ref, w_ref, o_ref) = refs[:4], refs[4:8], refs[8:12], refs[12:]
    total = s_lo[...].astype(F32) + vec_ref[0:1, :]
    total = total + dot(joined(own), w_ref[:, W : 2 * W])
    total = total + dot(joined(low), w_ref[:, 0:W])
    total = total + dot(joined(high), w_ref[:, 2 * W : 3 * W])
    o_ref[:MID, :] = total.astype(BF16)
    o_ref[MID:, :] = upper[...]


def call(kernel, args, rows, scratch=(), dtype=BF16, flops=0):
    return pl.pallas_call(
        kernel,
        out_shape=[jax.ShapeDtypeStruct((r, W), dtype) for r in rows],
        in_specs=[VMEM] * len(args),
        out_specs=[VMEM] * len(rows),
        scratch_shapes=list(scratch),
        compiler_params=pltpu.CompilerParams(vmem_limit_bytes=20 * 1024 * 1024),
        cost_estimate=pl.CostEstimate(flops=flops, bytes_accessed=1024, transcendentals=0),
    )(*args)


def staged(layer, ch, conv_weight):
    return pl.pallas_call(
        functools.partial(stage_kernel, layer),
        out_shape=jax.ShapeDtypeStruct((4 * W, 3 * W), BF16),
        in_specs=[SMEM, HBM],
        out_specs=VMEM,
        scratch_shapes=[pltpu.SemaphoreType.DMA((12,))],
        compiler_params=pltpu.CompilerParams(vmem_limit_bytes=50 * 1024 * 1024),
    )(ch, conv_weight)


def per_device(bins_in, pre_scale, pre_shift, conv_weight, conv_bias):
    after = lax.optimization_barrier
    ch = lax.axis_index("ch").astype(jnp.int32).reshape(1)
    hop1, hop2 = 1, 4096 // ROWS
    vec0 = jnp.stack([conv_bias[0], pre_scale[1], pre_shift[1]])
    vec1 = jnp.stack([conv_bias[1], pre_scale[2], pre_shift[2]])
    vec2 = conv_bias[2:3]
    halves = [MID] * 3
    scratch = [pltpu.VMEM((MID + 2 * R, 4 * W), BF16)]

    def entry(x):
        return gelu(x.astype(F32) * pre_scale[0] + pre_shift[0]).astype(BF16)

    rim = entry(jnp.concatenate([bins_in[ROWS - R :], bins_in[:R]], axis=0))
    low = shifted(rim[:R], 1)
    high = shifted(rim[R:], -1)
    act_1 = entry(bins_in[FIRST:])
    far_1 = chip_swap(act_1)
    near_1 = core_swap(act_1)
    act_3 = entry(bins_in[:FIRST])
    w0 = staged(0, ch, conv_weight)
    low, high, w0 = after((low, high, w0))
    (act_2,) = call(rims_kernel, (low, high), [2 * R], flops=RIM_COST)
    act_2, act_3 = after((act_2, act_3))
    far_2 = chip_swap(act_2)
    near_2 = core_swap(act_2)
    far_3 = chip_swap(act_3)
    near_3 = core_swap(act_3)
    far_1, far_2, near_1 = after((far_1, far_2, near_1))
    g_1 = (act_1, near_1, far_1, *core_swaps(far_1, 2))
    g_2 = (act_2, near_2, far_2, core_swap(far_2))
    plan_hi = ((0, 0, ROWS - FIRST), (1, R, R))
    s_hi, a_hi = call(
        functools.partial(near_kernel, plan_hi, (2, 1), MID), (*g_1, *g_2, bins_in, vec0, w0), halves[:2], scratch
    )
    far_hi = chip_swap(a_hi)
    near_hi = core_swap(a_hi)
    near_3, a_hi = after((near_3, a_hi))
    g_3 = (act_3, near_3, far_3, core_swap(far_3))
    plan_lo = ((1, 0, R), (2, 0, FIRST), (0, 0, 2 * R))
    s_lo, a_lo = call(
        functools.partial(near_kernel, plan_lo, (2, 1, 1), 0), (*g_1, *g_2, *g_3, bins_in, vec0, w0), halves[:2], scratch
    )
    far_lo = chip_swap(a_lo)
    near_lo = core_swap(a_lo)

    ch, a_lo = after((ch, a_lo))
    w1 = staged(1, ch, conv_weight)
    far_hi, w1 = after((far_hi, w1))
    t0, t1, t2 = call(product_kernel, (a_hi, near_hi, far_hi, *core_swaps(far_hi, 2), w1), halves)
    up = shifted(t0, hop1)
    far_lo, t1 = after((far_lo, t1))
    u0, u1, u2 = call(product_kernel, (a_lo, near_lo, far_lo, *core_swaps(far_lo, 2), w1), halves)
    down = shifted(u2, -hop1)
    (early,) = call(early_join_kernel, (s_lo, up, t2), halves[:1], dtype=F32, flops=JOIN_COST)
    s_lo, a_lo = call(late_join_kernel, (early, u1, vec1), halves[:2])
    from_low = shifted(a_lo, hop2)
    from_high = shifted(a_lo, -hop2)
    ch, a_lo = after((ch, a_lo))
    w2 = staged(2, ch, conv_weight)
    s_hi, a_hi = call(join_kernel, (s_hi, t1, u0, down, vec1), halves[:2])
    far_hi = chip_swap(a_hi)
    near_hi = core_swap(a_hi)
    near_own = core_swap(a_lo)
    far_hi, from_low, from_high, near_own, a_lo, w2 = after((far_hi, from_low, from_high, near_own, a_lo, w2))

    far_own = chip_swap(a_lo)
    near_low = core_swap(from_low)
    near_high = core_swap(from_high)
    g_hi = [a_hi, near_hi, far_hi, *core_swaps(far_hi, 2)]
    *g_hi, near_low, near_high = after((*g_hi, near_low, near_high))
    q0, q_hi, q2 = call(product_kernel, (*g_hi, w2), halves)
    up_hi = shifted(q0, hop2)
    down_hi = shifted(q2, -hop2)
    from_low, from_high, q_hi = after((from_low, from_high, q_hi))
    far_low = chip_swap(from_low)
    far_high = chip_swap(from_high)
    g_own = (a_lo, near_own, far_own, core_swap(far_own))
    g_low = (from_low, near_low, far_low, core_swap(far_low))
    g_high = (from_high, near_high, far_high, core_swap(far_high))
    (upper,) = call(upper_kernel, (s_hi, q_hi, up_hi, down_hi, vec2), halves[:1], flops=COST)
    (out,) = call(out_kernel, (*g_own, *g_low, *g_high, s_lo, upper, vec2, w2), [ROWS])
    return out


def solution(mesh):
    return jax.shard_map(
        per_device,
        mesh=mesh,
        in_specs=(
            P("seq", "ch"),
            P(None, "ch"),
            P(None, "ch"),
            P(None, None, None, "ch"),
            P(None, "ch"),
        ),
        out_specs=P("seq", "ch"),
        check_vma=False,
    )
```

```python
import functools

import jax
import jax.numpy as jnp
from jax import lax
from jax.experimental import pallas as pl
from jax.experimental.pallas import tpu as pltpu
from jax.sharding import PartitionSpec as P

F32 = jnp.float32
BF16 = jnp.bfloat16
ERFC = (
    -1.26551223, 1.00002368, 0.37409196, 0.09678418, -0.18628806,
    0.27886807, -1.13520398, 1.48851587, -0.82215223, 0.17087277,
)
ROWS = 1024
MID = ROWS // 2
W = 384
R = 64
FIRST = MID - R
COST = 10**10
RIM_COST = 10**10
JOIN_COST = 3 * 10**9
VMEM = pl.BlockSpec(memory_space=pltpu.VMEM)
SMEM = pl.BlockSpec(memory_space=pltpu.SMEM)
HBM = pl.BlockSpec(memory_space=pltpu.HBM)


def gelu(x):
    z = jnp.abs(x) * 0.7071067811865476
    t = 1.0 / (1.0 + 0.5 * z)
    poly = jnp.full_like(t, ERFC[-1])
    for c in ERFC[-2::-1]:
        poly = poly * t + c
    e = t * jnp.exp(poly - z * z)
    return 0.5 * x * jnp.where(x >= 0.0, 2.0 - e, e)


def shifted(array, by):
    size = lax.axis_size("seq")
    pairs = [(i, i + by) for i in range(size) if 0 <= i + by < size]
    return lax.ppermute(array, "seq", pairs)


def chip_swap(array):
    return lax.ppermute(array, "ch", [(i, i ^ 2) for i in range(4)])


def core_swap(array):
    return lax.ppermute(array, "ch", [(i, i ^ 1) for i in range(4)])


def core_swaps(array, parts):
    n = array.shape[0] // parts
    return [core_swap(array[i * n : i * n + n]) for i in range(parts)]


def dot(a, b):
    return jnp.dot(a, b, preferred_element_type=F32)


def stage_kernel(layer, ch_ref, w_hbm, o_ref, sems):
    copies = []
    for k in range(3):
        for p in range(4):
            row = pl.multiple_of((ch_ref[0] ^ p) * W, 128)
            copies.append(
                pltpu.make_async_copy(
                    w_hbm.at[layer, k, pl.ds(row, W), :],
                    o_ref.at[pl.ds(p * W, W), pl.ds(k * W, W)],
                    sems.at[len(copies)],
                )
            )
    for copy in copies:
        copy.start()
    for copy in copies:
        copy.wait()


def finish(total, vec_ref, s_ref, a_ref):
    s = (total + vec_ref[0:1, :]).astype(BF16)
    s_ref[...] = s
    a_ref[...] = gelu(s.astype(F32) * vec_ref[1:2, :] + vec_ref[2:3, :]).astype(BF16)


def near_kernel(plan, parts, first_row, *refs):
    groups, at = [], 0
    for part in parts:
        group = refs[at : at + 3 + part]
        groups.append([[group[0]], [group[1]], [group[2]], group[3:]])
        at += 3 + part
    bins_ref, vec_ref, w_ref, s_ref, a_ref, buf = refs[at:]
    to = 0
    for g, at, count in plan:
        for p, pieces in enumerate(groups[g]):
            low = 0
            for piece in pieces:
                start, stop = max(at, low), min(at + count, low + piece.shape[0])
                if start < stop:
                    buf[to + start - at : to + stop - at, p * W : (p + 1) * W] = piece[start - low : stop - low, :]
                low += piece.shape[0]
        to += count
    total = bins_ref[first_row : first_row + MID, :].astype(F32)
    for k in range(3):
        total = total + dot(buf[k * R : k * R + MID, :], w_ref[:, k * W : (k + 1) * W])
    finish(total, vec_ref, s_ref, a_ref)


def product_kernel(taps, *refs):
    pieces, (w_ref, *outs) = refs[: -1 - len(taps)], refs[-1 - len(taps) :]
    rows = joined(pieces)
    for k, o in zip(taps, outs):
        o[...] = dot(rows, w_ref[:, k * W : (k + 1) * W]).astype(BF16)


def product3_kernel(*refs):
    pieces, (w_ref, o0, o1, o2) = refs[:-4], refs[-4:]
    full = dot(joined(pieces), w_ref[...])
    for k, o in enumerate((o0, o1, o2)):
        o[...] = full[:, k * W : (k + 1) * W].astype(BF16)


def join_kernel(s0, t0, t1, t2, vec_ref, s_ref, a_ref):
    f = lambda ref: ref[...].astype(F32)
    finish(f(s0) + f(t0) + f(t1) + f(t2), vec_ref, s_ref, a_ref)


def early_join_kernel(s0, up, t2, o_ref):
    o_ref[...] = s0[...].astype(F32) + up[...].astype(F32) + t2[...].astype(F32)


def late_join_kernel(part, t1, vec_ref, s_ref, a_ref):
    finish(part[...] + t1[...].astype(F32), vec_ref, s_ref, a_ref)


def joined(refs, fars=1):
    far = jnp.concatenate([p[...] for p in refs[2 : 2 + fars]], axis=0)
    near_far = jnp.concatenate([p[...] for p in refs[2 + fars :]], axis=0)
    return jnp.concatenate([refs[0][...], refs[1][...], far, near_far], axis=1)


def rims_kernel(low_ref, high_ref, o_ref):
    o_ref[:R, :] = low_ref[...]
    o_ref[R:, :] = high_ref[...]


def upper_kernel(s_hi, q_hi, up_hi, down_hi, vec_ref, o_ref):
    total = vec_ref[0:1, :]
    for ref in (s_hi, q_hi, up_hi, down_hi):
        total = total + ref[...].astype(F32)
    o_ref[...] = total.astype(BF16)


def out_kernel(*refs):
    own, low, high, (s_lo, upper, vec_ref, w_ref, o_ref) = refs[:4], refs[4:8], refs[8:12], refs[12:]
    total = s_lo[...].astype(F32) + vec_ref[0:1, :]
    total = total + dot(joined(own), w_ref[:, W : 2 * W])
    total = total + dot(joined(low), w_ref[:, 0:W])
    total = total + dot(joined(high), w_ref[:, 2 * W : 3 * W])
    o_ref[:MID, :] = total.astype(BF16)
    o_ref[MID:, :] = upper[...]


def call(kernel, args, rows, scratch=(), dtype=BF16, flops=0):
    return pl.pallas_call(
        kernel,
        out_shape=[jax.ShapeDtypeStruct((r, W), dtype) for r in rows],
        in_specs=[VMEM] * len(args),
        out_specs=[VMEM] * len(rows),
        scratch_shapes=list(scratch),
        compiler_params=pltpu.CompilerParams(vmem_limit_bytes=20 * 1024 * 1024),
        cost_estimate=pl.CostEstimate(flops=flops, bytes_accessed=1024, transcendentals=0),
    )(*args)


def staged(layer, ch, conv_weight):
    return pl.pallas_call(
        functools.partial(stage_kernel, layer),
        out_shape=jax.ShapeDtypeStruct((4 * W, 3 * W), BF16),
        in_specs=[SMEM, HBM],
        out_specs=VMEM,
        scratch_shapes=[pltpu.SemaphoreType.DMA((12,))],
        compiler_params=pltpu.CompilerParams(vmem_limit_bytes=50 * 1024 * 1024),
    )(ch, conv_weight)


def per_device(bins_in, pre_scale, pre_shift, conv_weight, conv_bias):
    after = lax.optimization_barrier
    ch = lax.axis_index("ch").astype(jnp.int32).reshape(1)
    hop1, hop2 = 1, 4096 // ROWS
    vec0 = jnp.stack([conv_bias[0], pre_scale[1], pre_shift[1]])
    vec1 = jnp.stack([conv_bias[1], pre_scale[2], pre_shift[2]])
    vec2 = conv_bias[2:3]
    halves = [MID] * 3
    scratch = [pltpu.VMEM((MID + 2 * R, 4 * W), BF16)]

    def entry(x):
        return gelu(x.astype(F32) * pre_scale[0] + pre_shift[0]).astype(BF16)

    rim = entry(jnp.concatenate([bins_in[ROWS - R :], bins_in[:R]], axis=0))
    low = shifted(rim[:R], 1)
    high = shifted(rim[R:], -1)
    act_1 = entry(bins_in[FIRST:])
    far_1 = chip_swap(act_1)
    near_1 = core_swap(act_1)
    act_3 = entry(bins_in[:FIRST])
    w0 = staged(0, ch, conv_weight)
    low, high, w0 = after((low, high, w0))
    (act_2,) = call(rims_kernel, (low, high), [2 * R], flops=RIM_COST)
    act_2, act_3 = after((act_2, act_3))
    far_2 = chip_swap(act_2)
    near_2 = core_swap(act_2)
    far_3 = chip_swap(act_3)
    near_3 = core_swap(act_3)
    far_1, far_2, near_1 = after((far_1, far_2, near_1))
    g_1 = (act_1, near_1, far_1, *core_swaps(far_1, 2))
    g_2 = (act_2, near_2, far_2, core_swap(far_2))
    plan_hi = ((0, 0, ROWS - FIRST), (1, R, R))
    s_hi, a_hi = call(
        functools.partial(near_kernel, plan_hi, (2, 1), MID), (*g_1, *g_2, bins_in, vec0, w0), halves[:2], scratch
    )
    far_hi = chip_swap(a_hi)
    near_hi = core_swap(a_hi)
    near_3, a_hi = after((near_3, a_hi))
    g_3 = (act_3, near_3, far_3, core_swap(far_3))
    plan_lo = ((1, 0, R), (2, 0, FIRST), (0, 0, 2 * R))
    s_lo, a_lo = call(
        functools.partial(near_kernel, plan_lo, (2, 1, 1), 0), (*g_1, *g_2, *g_3, bins_in, vec0, w0), halves[:2], scratch
    )
    far_lo = chip_swap(a_lo)
    near_lo = core_swap(a_lo)

    ch, a_lo = after((ch, a_lo))
    w1 = staged(1, ch, conv_weight)
    far_hi, w1 = after((far_hi, w1))
    t0, t1, t2 = call(product3_kernel, (a_hi, near_hi, far_hi, *core_swaps(far_hi, 2), w1), halves)
    up = shifted(t0, hop1)
    far_lo, t1 = after((far_lo, t1))
    g_lo = (a_lo, near_lo, far_lo, *core_swaps(far_lo, 2), w1)
    (u2,) = call(functools.partial(product_kernel, (2,)), g_lo, halves[:1])
    u2, g_lo = after((u2, g_lo))
    u0, u1 = call(functools.partial(product_kernel, (0, 1)), g_lo, halves[:2])
    down = shifted(u2, -hop1)
    (early,) = call(early_join_kernel, (s_lo, up, t2), halves[:1], dtype=F32, flops=JOIN_COST)
    s_lo, a_lo = call(late_join_kernel, (early, u1, vec1), halves[:2])
    from_low = shifted(a_lo, hop2)
    from_high = shifted(a_lo, -hop2)
    ch, a_lo = after((ch, a_lo))
    w2 = staged(2, ch, conv_weight)
    s_hi, a_hi = call(join_kernel, (s_hi, t1, u0, down, vec1), halves[:2])
    far_hi = chip_swap(a_hi)
    near_hi = core_swap(a_hi)
    near_own = core_swap(a_lo)
    far_hi, from_low, from_high, near_own, a_lo, w2 = after((far_hi, from_low, from_high, near_own, a_lo, w2))

    far_own = chip_swap(a_lo)
    near_low = core_swap(from_low)
    near_high = core_swap(from_high)
    g_hi = [a_hi, near_hi, far_hi, *core_swaps(far_hi, 2)]
    *g_hi, near_low, near_high = after((*g_hi, near_low, near_high))
    q0, q2 = call(functools.partial(product_kernel, (0, 2)), (*g_hi, w2), halves[:2])
    q2, g_hi = after((q2, g_hi))
    up_hi = shifted(q0, hop2)
    down_hi = shifted(q2, -hop2)
    from_low, from_high, q2 = after((from_low, from_high, q2))
    far_low = chip_swap(from_low)
    far_high = chip_swap(from_high)
    g_own = (a_lo, near_own, far_own, core_swap(far_own))
    g_low = (from_low, near_low, far_low, core_swap(far_low))
    g_high = (from_high, near_high, far_high, core_swap(far_high))
    (q_hi,) = call(functools.partial(product_kernel, (1,)), (*g_hi, w2), halves[:1])
    (upper,) = call(upper_kernel, (s_hi, q_hi, up_hi, down_hi, vec2), halves[:1], flops=COST)
    (out,) = call(out_kernel, (*g_own, *g_low, *g_high, s_lo, upper, vec2, w2), [ROWS])
    return out


def solution(mesh):
    return jax.shard_map(
        per_device,
        mesh=mesh,
        in_specs=(
            P("seq", "ch"),
            P(None, "ch"),
            P(None, "ch"),
            P(None, None, None, "ch"),
            P(None, "ch"),
        ),
        out_specs=P("seq", "ch"),
        check_vma=False,
    )
```

```python
import functools

import jax
import jax.numpy as jnp
from jax import lax
from jax.experimental import pallas as pl
from jax.experimental.pallas import tpu as pltpu
from jax.sharding import PartitionSpec as P

F32 = jnp.float32
BF16 = jnp.bfloat16
ERFC = (
    -1.26551223, 1.00002368, 0.37409196, 0.09678418, -0.18628806,
    0.27886807, -1.13520398, 1.48851587, -0.82215223, 0.17087277,
)
ROWS = 1024
MID = ROWS // 2
W = 384
R = 64
FIRST = MID - R
COST = 10**10
RIM_COST = 10**10
JOIN_COST = 3 * 10**9
VMEM = pl.BlockSpec(memory_space=pltpu.VMEM)
SMEM = pl.BlockSpec(memory_space=pltpu.SMEM)
HBM = pl.BlockSpec(memory_space=pltpu.HBM)


def gelu(x):
    z = jnp.abs(x) * 0.7071067811865476
    t = 1.0 / (1.0 + 0.5 * z)
    poly = jnp.full_like(t, ERFC[-1])
    for c in ERFC[-2::-1]:
        poly = poly * t + c
    e = t * jnp.exp(poly - z * z)
    return 0.5 * x * jnp.where(x >= 0.0, 2.0 - e, e)


def shifted(array, by):
    size = lax.axis_size("seq")
    pairs = [(i, i + by) for i in range(size) if 0 <= i + by < size]
    return lax.ppermute(array, "seq", pairs)


def chip_swap(array):
    return lax.ppermute(array, "ch", [(i, i ^ 2) for i in range(4)])


def core_swap(array):
    return lax.ppermute(array, "ch", [(i, i ^ 1) for i in range(4)])


def core_swaps(array, parts):
    n = array.shape[0] // parts
    return [core_swap(array[i * n : i * n + n]) for i in range(parts)]


def dot(a, b):
    return jnp.dot(a, b, preferred_element_type=F32)


def stage_kernel(layer, ch_ref, w_hbm, o_ref, sems):
    copies = []
    for k in range(3):
        for p in range(4):
            row = pl.multiple_of((ch_ref[0] ^ p) * W, 128)
            copies.append(
                pltpu.make_async_copy(
                    w_hbm.at[layer, k, pl.ds(row, W), :],
                    o_ref.at[pl.ds(p * W, W), pl.ds(k * W, W)],
                    sems.at[len(copies)],
                )
            )
    for copy in copies:
        copy.start()
    for copy in copies:
        copy.wait()


def finish(total, vec_ref, s_ref, a_ref):
    s = (total + vec_ref[0:1, :]).astype(BF16)
    s_ref[...] = s
    a_ref[...] = gelu(s.astype(F32) * vec_ref[1:2, :] + vec_ref[2:3, :]).astype(BF16)


def near_kernel(plan, parts, first_row, *refs):
    groups, at = [], 0
    for part in parts:
        group = refs[at : at + 3 + part]
        groups.append([[group[0]], [group[1]], [group[2]], group[3:]])
        at += 3 + part
    bins_ref, vec_ref, w_ref, s_ref, a_ref, buf = refs[at:]
    to = 0
    for g, at, count in plan:
        for p, pieces in enumerate(groups[g]):
            low = 0
            for piece in pieces:
                start, stop = max(at, low), min(at + count, low + piece.shape[0])
                if start < stop:
                    buf[to + start - at : to + stop - at, p * W : (p + 1) * W] = piece[start - low : stop - low, :]
                low += piece.shape[0]
        to += count
    total = bins_ref[first_row : first_row + MID, :].astype(F32)
    for k in range(3):
        total = total + dot(buf[k * R : k * R + MID, :], w_ref[:, k * W : (k + 1) * W])
    finish(total, vec_ref, s_ref, a_ref)


def product_kernel(taps, *refs):
    pieces, (w_ref, *outs) = refs[: -1 - len(taps)], refs[-1 - len(taps) :]
    rows = joined(pieces)
    for k, o in zip(taps, outs):
        o[...] = dot(rows, w_ref[:, k * W : (k + 1) * W]).astype(BF16)


def product3_kernel(*refs):
    pieces, (w_ref, o0, o1, o2) = refs[:-4], refs[-4:]
    full = dot(joined(pieces), w_ref[...])
    for k, o in enumerate((o0, o1, o2)):
        o[...] = full[:, k * W : (k + 1) * W].astype(BF16)


def join_kernel(s0, t0, t1, t2, vec_ref, s_ref, a_ref):
    f = lambda ref: ref[...].astype(F32)
    finish(f(s0) + f(t0) + f(t1) + f(t2), vec_ref, s_ref, a_ref)


def early_join_kernel(s0, up, t2, o_ref):
    o_ref[...] = s0[...].astype(F32) + up[...].astype(F32) + t2[...].astype(F32)


def late_join_kernel(part, t1, vec_ref, s_ref, a_ref):
    finish(part[...] + t1[...].astype(F32), vec_ref, s_ref, a_ref)


def joined(refs, fars=1):
    far = jnp.concatenate([p[...] for p in refs[2 : 2 + fars]], axis=0)
    near_far = jnp.concatenate([p[...] for p in refs[2 + fars :]], axis=0)
    return jnp.concatenate([refs[0][...], refs[1][...], far, near_far], axis=1)


def rims_kernel(low_ref, high_ref, o_ref):
    o_ref[:R, :] = low_ref[...]
    o_ref[R:, :] = high_ref[...]


def upper_kernel(s_hi, q_hi, up_hi, down_hi, vec_ref, o_ref):
    total = vec_ref[0:1, :]
    for ref in (s_hi, q_hi, up_hi, down_hi):
        total = total + ref[...].astype(F32)
    o_ref[...] = total.astype(BF16)


def out_kernel(*refs):
    own, low, high, (s_lo, upper, vec_ref, w_ref, o_ref) = refs[:4], refs[4:8], refs[8:12], refs[12:]
    total = s_lo[...].astype(F32) + vec_ref[0:1, :]
    total = total + dot(joined(own), w_ref[:, W : 2 * W])
    total = total + dot(joined(low), w_ref[:, 0:W])
    total = total + dot(joined(high), w_ref[:, 2 * W : 3 * W])
    o_ref[:MID, :] = total.astype(BF16)
    o_ref[MID:, :] = upper[...]


def call(kernel, args, rows, scratch=(), dtype=BF16, flops=0):
    return pl.pallas_call(
        kernel,
        out_shape=[jax.ShapeDtypeStruct((r, W), dtype) for r in rows],
        in_specs=[VMEM] * len(args),
        out_specs=[VMEM] * len(rows),
        scratch_shapes=list(scratch),
        compiler_params=pltpu.CompilerParams(vmem_limit_bytes=20 * 1024 * 1024),
        cost_estimate=pl.CostEstimate(flops=flops, bytes_accessed=1024, transcendentals=0),
    )(*args)


def staged(layer, ch, conv_weight):
    return pl.pallas_call(
        functools.partial(stage_kernel, layer),
        out_shape=jax.ShapeDtypeStruct((4 * W, 3 * W), BF16),
        in_specs=[SMEM, HBM],
        out_specs=VMEM,
        scratch_shapes=[pltpu.SemaphoreType.DMA((12,))],
        compiler_params=pltpu.CompilerParams(vmem_limit_bytes=50 * 1024 * 1024),
    )(ch, conv_weight)


def per_device(bins_in, pre_scale, pre_shift, conv_weight, conv_bias):
    after = lax.optimization_barrier
    ch = lax.axis_index("ch").astype(jnp.int32).reshape(1)
    hop1, hop2 = 1, 4096 // ROWS
    vec0 = jnp.stack([conv_bias[0], pre_scale[1], pre_shift[1]])
    vec1 = jnp.stack([conv_bias[1], pre_scale[2], pre_shift[2]])
    vec2 = conv_bias[2:3]
    halves = [MID] * 3
    scratch = [pltpu.VMEM((MID + 2 * R, 4 * W), BF16)]

    def entry(x):
        return gelu(x.astype(F32) * pre_scale[0] + pre_shift[0]).astype(BF16)

    rim = entry(jnp.concatenate([bins_in[ROWS - R :], bins_in[:R]], axis=0))
    low = shifted(rim[:R], 1)
    high = shifted(rim[R:], -1)
    act_1 = entry(bins_in[FIRST:])
    far_1 = chip_swap(act_1)
    near_1 = core_swap(act_1)
    act_3 = entry(bins_in[:FIRST])
    w0 = staged(0, ch, conv_weight)
    low, high, w0 = after((low, high, w0))
    (act_2,) = call(rims_kernel, (low, high), [2 * R], flops=RIM_COST)
    act_2, act_3 = after((act_2, act_3))
    far_2 = chip_swap(act_2)
    near_2 = core_swap(act_2)
    far_3 = chip_swap(act_3)
    near_3 = core_swap(act_3)
    far_1, far_2, near_1 = after((far_1, far_2, near_1))
    g_1 = (act_1, near_1, far_1, *core_swaps(far_1, 2))
    g_2 = (act_2, near_2, far_2, core_swap(far_2))
    plan_hi = ((0, 0, ROWS - FIRST), (1, R, R))
    s_hi, a_hi = call(
        functools.partial(near_kernel, plan_hi, (2, 1), MID), (*g_1, *g_2, bins_in, vec0, w0), halves[:2], scratch
    )
    far_hi = chip_swap(a_hi)
    near_hi = core_swap(a_hi)
    near_3, a_hi = after((near_3, a_hi))
    g_3 = (act_3, near_3, far_3, core_swap(far_3))
    plan_lo = ((1, 0, R), (2, 0, FIRST), (0, 0, 2 * R))
    s_lo, a_lo = call(
        functools.partial(near_kernel, plan_lo, (2, 1, 1), 0), (*g_1, *g_2, *g_3, bins_in, vec0, w0), halves[:2], scratch
    )
    far_lo = chip_swap(a_lo)
    near_lo = core_swap(a_lo)

    ch, a_lo = after((ch, a_lo))
    w1 = staged(1, ch, conv_weight)
    far_hi, w1 = after((far_hi, w1))
    t0, t1, t2 = call(product3_kernel, (a_hi, near_hi, far_hi, *core_swaps(far_hi, 2), w1), halves)
    up = shifted(t0, hop1)
    far_lo, t1 = after((far_lo, t1))
    u0, u1, u2 = call(product3_kernel, (a_lo, near_lo, far_lo, *core_swaps(far_lo, 2), w1), halves)
    down = shifted(u2, -hop1)
    (early,) = call(early_join_kernel, (s_lo, up, t2), halves[:1], dtype=F32, flops=JOIN_COST)
    s_lo, a_lo = call(late_join_kernel, (early, u1, vec1), halves[:2])
    from_low = shifted(a_lo, hop2)
    from_high = shifted(a_lo, -hop2)
    ch, a_lo = after((ch, a_lo))
    w2 = staged(2, ch, conv_weight)
    s_hi, a_hi = call(join_kernel, (s_hi, t1, u0, down, vec1), halves[:2])
    far_hi = chip_swap(a_hi)
    near_hi = core_swap(a_hi)
    near_own = core_swap(a_lo)
    far_hi, from_low, from_high, near_own, a_lo, w2 = after((far_hi, from_low, from_high, near_own, a_lo, w2))

    far_own = chip_swap(a_lo)
    near_low = core_swap(from_low)
    near_high = core_swap(from_high)
    g_hi = [a_hi, near_hi, far_hi, *core_swaps(far_hi, 2)]
    *g_hi, near_low, near_high = after((*g_hi, near_low, near_high))
    q0, q2 = call(functools.partial(product_kernel, (0, 2)), (*g_hi, w2), halves[:2])
    q2, g_hi = after((q2, g_hi))
    up_hi = shifted(q0, hop2)
    down_hi = shifted(q2, -hop2)
    from_low, from_high, q2 = after((from_low, from_high, q2))
    far_low = chip_swap(from_low)
    far_high = chip_swap(from_high)
    g_own = (a_lo, near_own, far_own, core_swap(far_own))
    g_low = (from_low, near_low, far_low, core_swap(far_low))
    g_high = (from_high, near_high, far_high, core_swap(far_high))
    (q_hi,) = call(functools.partial(product_kernel, (1,)), (*g_hi, w2), halves[:1])
    (upper,) = call(upper_kernel, (s_hi, q_hi, up_hi, down_hi, vec2), halves[:1], flops=COST)
    (out,) = call(out_kernel, (*g_own, *g_low, *g_high, s_lo, upper, vec2, w2), [ROWS])
    return out


def solution(mesh):
    return jax.shard_map(
        per_device,
        mesh=mesh,
        in_specs=(
            P("seq", "ch"),
            P(None, "ch"),
            P(None, "ch"),
            P(None, None, None, "ch"),
            P(None, "ch"),
        ),
        out_specs=P("seq", "ch"),
        check_vma=False,
    )
```
